32 devices in a mesh: group: 4 (over y, x), shard: 8 (over z, core).
Axes of the slice: x: 2, y: 2, z: 4, core: 2. Of those that a mesh axis runs over, the one named last changes fastest.
Arguments:
- node_features: bfloat16 [512, 49, 128], P(('group', 'shard')), may hold values from -6 to 6
- weight: bfloat16 [7, 128, 128], replicated, may hold values from -0.5 to 0.5
- wigner: bfloat16 [7, 13, 13, 4096], P(None, None, None, ('group', 'shard'))
- radial: float32 [7, 4096], P(None, ('group', 'shard')), may hold values from 0.3 to 3
- edge_src: int32 [4096], P(('group', 'shard')), may hold values from 0 to 35, as said below
- edge_dst: int32 [4096], P(('group', 'shard')), may hold values from 0 to 15
- send_index: int32 [320, 2], P(('group', 'shard')), may hold values from 0 to 15
- edge_count: int32 [32], P(('group', 'shard')), may hold values from 32 to 128, as said below
- grad_update: bfloat16 [512, 49, 128], P(('group', 'shard')), may hold values from -6 to 6
Outputs:
- update: bfloat16 [512, 49, 128], P(('group', 'shard'))
- grad_input: bfloat16 [512, 49, 128], P(('group', 'shard'))
- grad_weight: float32 [7, 128, 128], replicated
The draws below stay inside these ranges and needn't reach their ends.
Inputs may be any that keep to these rules, and one draw needn't show every extreme that they name: `edge_src`: A source of 16 or more names a halo slot of a direction whose sender exists, and for directions 0 to 7 also whose shard s - dc lies in the same row of 8 as s. `edge_count`: some device has all its edge slots live.
All inputs are finite; a program needn't handle non-finite values.
Results may differ from the reference program's by a relative error of at most 0.006.
Values may be sent and summed in bfloat16 or wider, within the bound.
No kernel may reach another device: no remote copies, remote signals or barrier semaphores. Data moves between devices by JAX's collectives and lax.ppermute only.
A program may use at most 128 MiB of HBM per device.

```python
import math
import jax
import jax.numpy as jnp
import numpy as np
from jax import lax

C = 128
COEF = 49
DIRS = 10
NODE_DEV = 16
SLOT = 2
EDGE_DEV = 128
NODES = 512
EDGES = 4096
N_GROUP = 4
N_SHARD = 8


def draw_wigner(key, part):
    degree = jnp.arange(7)[:, None, None, None]
    row = jnp.arange(13)[None, :, None, None]
    col = jnp.arange(13)[None, None, :, None]
    inside = ((row <= 2 * degree) & (col <= 2 * degree)).astype(jnp.float32)
    scale = 1.0 / jnp.sqrt(2.0 * degree + 1.0)
    values = jax.random.normal(key, (7, 13, 13, EDGES), jnp.float32)
    return (values * inside * scale).astype(jnp.bfloat16)


def draw_edge_src(key, part):
    keys = jax.random.split(key, 4)
    slot_id = jnp.arange(EDGES, dtype=jnp.int32)
    device = slot_id // EDGE_DEV
    group_at = device // N_SHARD
    shard_at = device % N_SHARD
    row_at = shard_at // 8
    col_at = shard_at % 8
    rows_all = N_SHARD // 8
    use_halo = jax.random.randint(keys[0], (EDGES,), 0, 2)
    way = jax.random.randint(keys[1], (EDGES,), 0, 10)
    place = jax.random.randint(keys[2], (EDGES,), 0, NODE_DEV // 8)
    local = jax.random.randint(keys[3], (EDGES,), 0, NODE_DEV)
    way_rows = jnp.array([-1, -1, -1, 0, 0, 1, 1, 1, 0, 0], jnp.int32)[way]
    way_cols = jnp.array([-1, 0, 1, -1, 1, -1, 0, 1, 0, 0], jnp.int32)[way]
    inner = (way < 8) & (row_at - way_rows >= 0) & (row_at - way_rows < rows_all) & (col_at - way_cols >= 0) & (col_at - way_cols < 8)
    outer = (way == 8) & (group_at >= 1) | (way == 9) & (group_at + 1 < N_GROUP)
    chosen = (use_halo == 1) & (inner | outer)
    return jnp.where(chosen, NODE_DEV + way * (NODE_DEV // 8) + place, local).astype(jnp.int32)


def draw_edge_count(key, part):
    keys = jax.random.split(key, 2)
    devices = N_GROUP * N_SHARD
    counts = jax.random.randint(keys[0], (devices,), EDGE_DEV // 4, EDGE_DEV + 1)
    full_at = jax.random.randint(keys[1], (), 0, devices)
    return counts.at[full_at].set(EDGE_DEV).astype(jnp.int32)


def plant(drawn, key, low, high):
    index_at = [jax.random.randint(jax.random.fold_in(key, axis), (), 0, length) for axis, length in enumerate(drawn.shape)]
    longest = drawn.shape.index(max(drawn.shape))
    beside = index_at[:longest] + [(index_at[longest] + 1) % drawn.shape[longest]] + index_at[longest + 1:]
    return drawn.at[tuple(index_at)].set(low).at[tuple(beside)].set(high)


def levels(key, shape, cuts, least, high):
    def one(dim, parts):
        steps = jax.random.uniform(jax.random.fold_in(jax.random.fold_in(key, 6), dim), (parts,), jnp.float32, least / len(cuts), high / len(cuts))
        return jnp.repeat(jnp.exp(steps), shape[dim] // parts).reshape((-1,) + (1,) * (len(shape) - dim - 1))

    level = one(*cuts[0])
    for cut in cuts[1:]:
        level = level * one(*cut)
    return level


def gaussian(stream_key, extent, deviation, limit, cuts=(), kind=jnp.bfloat16):
    entries = deviation * jax.random.normal(stream_key, extent, jnp.float32)
    if cuts:
        entries = entries * levels(stream_key, extent, cuts, -0.22, 0.18)
    return jnp.clip(entries, -limit, limit).astype(kind)


def setup_inputs(seed: int = 0) -> dict:
    streams_of = jax.random.split(jax.random.key(seed), 10)
    return {
        "node_features": gaussian(streams_of[0], (NODES, COEF, C), 1.0, 6.0, ((0, 32),)),
        "weight": gaussian(streams_of[1], (7, C, C), C ** -0.5, 0.5),
        "wigner": draw_wigner(jax.random.fold_in(streams_of[9], 71), 0),
        "radial": jnp.clip(jnp.exp(math.log(3.0) - 2.3025851 * jax.random.uniform(streams_of[3], (7, EDGES), jnp.float32) ** levels(streams_of[3], (7, EDGES), ((1, 32),), -0.2, 0.2)), 0.3, 3.0),
        "edge_src": draw_edge_src(jax.random.fold_in(streams_of[9], 71), 0),
        "edge_dst": plant(jax.random.randint(streams_of[5], (EDGES,), 0, NODE_DEV), jax.random.fold_in(streams_of[5], 1), 0, NODE_DEV - 1).astype(jnp.int32),
        "send_index": plant(jax.random.randint(streams_of[6], (N_GROUP * N_SHARD * DIRS, SLOT), 0, NODE_DEV), jax.random.fold_in(streams_of[6], 1), 0, NODE_DEV - 1).astype(jnp.int32),
        "edge_count": draw_edge_count(jax.random.fold_in(streams_of[9], 71), 0),
        "grad_update": gaussian(streams_of[8], (NODES, COEF, C), 1.0, 6.0, ((0, 32),)),
    }


coef_degree = np.array([l for l in range(7) for i in range(2 * l + 1)], np.int32)
coef_place = np.array([i for l in range(7) for i in range(2 * l + 1)], np.int32)
pad_index = np.array([[l * l + min(i, 2 * l) for i in range(13)] for l in range(7)], np.int32)
pad_mask = np.array([[1.0 if i <= 2 * l else 0.0 for i in range(13)] for l in range(7)], np.float32)
order_rows = [np.array([k for k in range(49) if abs(int(coef_place[k]) - int(coef_degree[k])) == mm], np.int32) for mm in range(7)]
restore = np.argsort(np.concatenate(order_rows)).astype(np.int32)
way_rows = np.array([-1, -1, -1, 0, 0, 1, 1, 1, 0, 0], np.int32)
way_cols = np.array([-1, 0, 1, -1, 1, -1, 0, 1, 0, 0], np.int32)
way_group = np.array([0, 0, 0, 0, 0, 0, 0, 0, 1, -1], np.int32)


def rotate_edges(wig_dev, feats, inverse):
    padded = feats[:, pad_index].astype(jnp.float32) * jnp.asarray(pad_mask)[None, :, :, None]
    form = "ljie,eljc->elic" if inverse else "lije,eljc->elic"
    out = jnp.einsum(form, wig_dev.astype(jnp.float32), padded)
    return out[:, coef_degree, coef_place]


def mix_orders(rot, weight, gain):
    pieces = []
    for mm in range(7):
        part = rot[:, order_rows[mm]].astype(jnp.float32)
        out = jnp.einsum("erc,cd->erd", part, weight[mm].astype(jnp.float32))
        pieces.append(out * gain[mm][:, None, None])
    return jnp.concatenate(pieces, axis=1)[:, restore]


def mix_grads(rot, grad_rot, weight, gain):
    pieces = []
    grads = []
    for mm in range(7):
        part = rot[:, order_rows[mm]].astype(jnp.float32)
        other = grad_rot[:, order_rows[mm]].astype(jnp.float32)
        scaled = (other * gain[mm][:, None, None]).astype(jnp.bfloat16)
        scaled = lax.optimization_barrier(scaled).astype(jnp.float32)
        grads.append(jnp.einsum("erc,erd->cd", part, scaled))
        out = jnp.einsum("erd,cd->erc", other, weight[mm].astype(jnp.float32))
        pieces.append(out * gain[mm][:, None, None])
    return jnp.stack(grads), jnp.concatenate(pieces, axis=1)[:, restore]


def reference(node_features, weight, wigner, radial, edge_src, edge_dst, send_index, edge_count, grad_update):
    devices = N_GROUP * N_SHARD
    sends = send_index.reshape(devices, DIRS, SLOT)
    wig = wigner.reshape(7, 13, 13, devices, EDGE_DEV)
    shard_step = jnp.asarray(8 * way_rows + way_cols)
    group_step = jnp.asarray(way_group)

    def visit(carry, device):
        grad_all, grad_w = carry
        src = lax.dynamic_slice_in_dim(edge_src, device * EDGE_DEV, EDGE_DEV)
        dst = lax.dynamic_slice_in_dim(edge_dst, device * EDGE_DEV, EDGE_DEV)
        gain = lax.dynamic_slice_in_dim(radial, device * EDGE_DEV, EDGE_DEV, 1)
        live = jnp.arange(EDGE_DEV, dtype=jnp.int32) < edge_count[device]
        gain = gain * live.astype(jnp.float32)[None, :]
        wig_dev = lax.dynamic_index_in_dim(wig, device, 3, False)
        local = src < NODE_DEV
        halo = jnp.maximum(src - NODE_DEV, 0)
        way = halo // SLOT
        place = halo % SLOT
        group_at = device // N_SHARD
        shard_at = device % N_SHARD
        sender_group = group_at - group_step[way]
        sender_shard = shard_at - shard_step[way]
        valid = local | ((sender_group >= 0) & (sender_group < N_GROUP) & (sender_shard >= 0) & (sender_shard < N_SHARD))
        sender = jnp.clip(sender_group, 0, N_GROUP - 1) * N_SHARD + jnp.clip(sender_shard, 0, N_SHARD - 1)
        remote = sends[sender, way, place]
        global_id = jnp.where(local, device * NODE_DEV + src, sender * NODE_DEV + remote).astype(jnp.int32)
        feats = node_features[global_id] * valid[:, None, None].astype(node_features.dtype)
        rot = rotate_edges(wig_dev, feats, False).astype(jnp.bfloat16)
        msg = mix_orders(rot, weight, gain).astype(jnp.bfloat16)
        back = rotate_edges(wig_dev, msg, True)
        update = jax.ops.segment_sum(back, dst, NODE_DEV).astype(jnp.bfloat16)
        grad_rows = lax.dynamic_slice_in_dim(grad_update, device * NODE_DEV, NODE_DEV)[dst]
        grad_rot = rotate_edges(wig_dev, grad_rows, False).astype(jnp.bfloat16)
        partial_w, grad_msg = mix_grads(rot, grad_rot, weight, gain)
        grad_src = rotate_edges(wig_dev, grad_msg.astype(jnp.bfloat16), True)
        grad_src = grad_src * valid[:, None, None].astype(jnp.float32)
        grad_all = grad_all.at[global_id].add(grad_src)
        return (grad_all, grad_w + partial_w), update

    start = (jnp.zeros((NODES, COEF, C), jnp.float32), jnp.zeros((7, C, C), jnp.float32))
    (grad_all, grad_w), updates = lax.scan(visit, start, jnp.arange(devices, dtype=jnp.int32))
    return updates.reshape(NODES, COEF, C), grad_all.astype(jnp.bfloat16), grad_w
```

```python
import functools

import jax
import jax.numpy as jnp
from jax import lax
from jax.experimental import pallas as pl
from jax.experimental.pallas import tpu as pltpu
from jax.sharding import PartitionSpec as P

F32, BF16 = jnp.float32, jnp.bfloat16
COLS = 8
LMAX = 6
COEF = (LMAX + 1) ** 2
ROW = 56
way_list = [(-1, -1), (-1, 0), (-1, 1), (0, -1), (0, 1), (1, -1), (1, 0), (1, 1)]


def exchanges(groups, shards):
    rows = shards // COLS
    found = []
    for dr, dc in [(0, 1), (1, -1), (1, 0), (1, 1)]:
        by = COLS * dr + dc
        for parity in (0, 1):
            pairs = []
            for s in range(shards):
                r, c = s // COLS, s % COLS
                if (r if dr else c) % 2 == parity and r + dr < rows and 0 <= c + dc < COLS:
                    pairs += [(s, s + by), (s + by, s)]
            if pairs:
                plus = way_list.index((dr, dc))
                found.append(("shard", plus, 7 - plus, "row" if dr else "col", parity, pairs))
    for parity in (0, 1):
        pairs = []
        for g in range(groups - 1):
            if g % 2 == parity:
                pairs += [(g, g + 1), (g + 1, g)]
        if pairs:
            found.append(("group", 8, 9, "group", parity, pairs))
    return found


def ways_of(exchange):
    _, plus, minus, coordinate, parity, _ = exchange
    if coordinate == "group":
        place = lax.axis_index("group")
    elif coordinate == "row":
        place = lax.div(lax.axis_index("shard"), COLS)
    else:
        place = lax.rem(lax.axis_index("shard"), COLS)
    lower = lax.rem(place, 2) == parity
    return jnp.where(lower, plus, minus), jnp.where(lower, minus, plus)


def dot(a, b, ca, cb):
    return lax.dot_general(a, b, (((ca,), (cb,)), ((), ())), preferred_element_type=F32)


def order_coefs(order):
    found = []
    for degree in range(order, LMAX + 1):
        centre = degree * degree + degree
        found += [centre] if order == 0 else [centre - order, centre + order]
    return found


def lanes(coef, edges):
    return slice(coef * edges, (coef + 1) * edges)


def dst_hot(dst, node_dev):
    edges = dst.shape[1]
    return (lax.broadcasted_iota(jnp.int32, (node_dev, edges), 0) == dst).astype(F32).astype(BF16)


def src_hot(src, node_dev, slot, ways, height):
    edges = src.shape[1]
    row = lax.broadcasted_iota(jnp.int32, (height, edges), 0)
    code = jnp.where(row < node_dev, row, -1)
    for number, way in enumerate(ways):
        for place in range(slot):
            code = jnp.where(
                row == node_dev + slot * number + place, node_dev + slot * way + place, code
            )
    return (code == src).astype(F32).astype(BF16)


def expand(wig_ref, degree, hots):
    width = 2 * degree + 1
    edges = wig_ref.shape[3]
    columns = [[] for _ in hots]
    for i in range(width):
        wig = wig_ref[degree, i].astype(F32)
        blocks = [[] for _ in hots]
        for j in range(width):
            row = jnp.broadcast_to(wig[j : j + 1], (16, edges)).astype(BF16)
            for number, hot in enumerate(hots):
                for start in range(0, hot.shape[0], 16):
                    blocks[number].append(hot[start : start + 16] * row)
        for number, block in enumerate(blocks):
            columns[number].append(jnp.concatenate(block, axis=0))
    return [jnp.concatenate(column, axis=1) for column in columns]


def spread(ref, scratch, base):
    for atom in range(ref.shape[0]):
        start = (base + atom) * ROW
        scratch[start : start + COEF, :] = ref[atom].astype(F32)


def rows_of(scratch, degree, atoms):
    pieces = []
    for coef in range(degree * degree, (degree + 1) * (degree + 1)):
        pieces.append(scratch[pl.ds(coef, atoms, stride=ROW), :].astype(BF16))
    return jnp.concatenate(pieces, axis=0)


def live_gain(radial_ref, count_ref):
    radial = radial_ref[...]
    at = lax.broadcasted_iota(jnp.int32, radial.shape, 1)
    return jnp.where(at < count_ref[0], radial, 0.0)


def send_kernel(plan, index_ref, nodes_ref, *outs):
    for exchange, out in zip(plan, outs):
        way, _ = ways_of(exchange)
        for place in range(out.shape[0]):
            out[place] = nodes_ref[index_ref[way, place]]


def grad_kernel(
    plan, slot, height,
    count_ref, src_ref, dst_ref, radial_ref, wig_ref, weight_ref, grad_ref,
    gs_ref, own_ref, *rest,
):
    backs, scratch, out_scratch = rest[:-2], rest[-2], rest[-1]
    node_dev = grad_ref.shape[0]
    edges = wig_ref.shape[3]
    gain = live_gain(radial_ref, count_ref)
    dst = dst_hot(dst_ref[...], node_dev)
    src = src_hot(src_ref[...], node_dev, slot, [ways_of(x)[1] for x in plan], height)
    spread(grad_ref, scratch, 0)
    for degree in range(LMAX, -1, -1):
        width = 2 * degree + 1
        base = degree * degree
        to_dst, to_src = expand(wig_ref, degree, [dst, src])
        gr = dot(rows_of(scratch, degree, node_dev), to_dst, 0, 0).astype(BF16)
        back = [None] * width
        for order in range(degree + 1):
            places = [degree] if order == 0 else [degree - order, degree + order]
            part = jnp.concatenate([gr[:, lanes(i, edges)] for i in places], axis=1)
            scale = jnp.concatenate([gain[order : order + 1]] * len(places), axis=1)
            scaled = (part.astype(F32) * scale).astype(BF16)
            mixed = (dot(weight_ref[order], part, 1, 0) * scale).astype(BF16)
            for number, i in enumerate(places):
                gs_ref[:, lanes(base + i, edges)] = scaled[:, lanes(number, edges)]
                back[i] = mixed[:, lanes(number, edges)]
        out = dot(to_src, jnp.concatenate(back, axis=1), 1, 1)
        for j in range(width):
            out_scratch[pl.ds(base + j, height, stride=ROW), :] = out[j * height : (j + 1) * height]
    for atom in range(node_dev):
        own_ref[atom] = out_scratch[atom * ROW : atom * ROW + COEF, :]
    for number, back_ref in enumerate(backs):
        for place in range(slot):
            start = (node_dev + slot * number + place) * ROW
            back_ref[place] = out_scratch[start : start + COEF, :].astype(BF16)


def rot_kernel(plan, slot, height, src_ref, wig_ref, nodes_ref, gs_ref, *rest):
    halos, (rot_ref, keep_ref, send_ref), (scratch,) = rest[:-4], rest[-4:-1], rest[-1:]
    node_dev = nodes_ref.shape[0]
    edges = wig_ref.shape[3]
    src = src_hot(src_ref[...], node_dev, slot, [ways_of(x)[1] for x in plan], height)
    used = node_dev + slot * len(plan)
    scratch[used * ROW :, :] = jnp.zeros(((height - used) * ROW, scratch.shape[1]), F32)
    spread(nodes_ref, scratch, 0)
    for number, halo in enumerate(halos):
        spread(halo, scratch, node_dev + slot * number)
    for degree in range(LMAX, -1, -1):
        [to_src] = expand(wig_ref, degree, [src])
        rot = dot(rows_of(scratch, degree, height), to_src, 0, 0).astype(BF16)
        rot_ref[:, degree * degree * edges : (degree + 1) * (degree + 1) * edges] = rot
    parts = []
    for order in range(LMAX + 1):
        coefs = order_coefs(order)
        left = jnp.concatenate([rot_ref[:, lanes(k, edges)] for k in coefs], axis=1)
        right = jnp.concatenate([gs_ref[:, lanes(k, edges)] for k in coefs], axis=1)
        parts.append(dot(left, right, 1, 1))
    whole = jnp.concatenate(parts, axis=0)
    half = whole.shape[0] // 2
    first = lax.rem(lax.axis_index("shard"), 2) == 0
    keep_ref[...] = jnp.where(first, whole[:half], whole[half:])
    send_ref[...] = jnp.where(first, whole[half:], whole[:half]).astype(BF16)


def update_kernel(count_ref, dst_ref, radial_ref, wig_ref, weight_ref, rot_ref, out_ref, scratch):
    node_dev = out_ref.shape[0]
    edges = wig_ref.shape[3]
    gain = live_gain(radial_ref, count_ref)
    dst = dst_hot(dst_ref[...], node_dev)
    for degree in range(LMAX + 1):
        width = 2 * degree + 1
        base = degree * degree
        [to_dst] = expand(wig_ref, degree, [dst])
        msg = [None] * width
        for order in range(degree + 1):
            places = [degree] if order == 0 else [degree - order, degree + order]
            part = jnp.concatenate([rot_ref[:, lanes(base + i, edges)] for i in places], axis=1)
            scale = jnp.concatenate([gain[order : order + 1]] * len(places), axis=1)
            mixed = (dot(weight_ref[order], part, 0, 0) * scale).astype(BF16)
            for number, i in enumerate(places):
                msg[i] = mixed[:, lanes(number, edges)]
        out = dot(to_dst, jnp.concatenate(msg, axis=1), 1, 1)
        for j in range(width):
            scratch[pl.ds(base + j, node_dev, stride=ROW), :] = out[j * node_dev : (j + 1) * node_dev]
    for atom in range(node_dev):
        out_ref[atom] = scratch[atom * ROW : atom * ROW + COEF, :].astype(BF16)


def finish_kernel(plan, index_ref, own_ref, *rest):
    backs, out_ref, scratch = rest[:-2], rest[-2], rest[-1]
    scratch[...] = own_ref[...]
    for exchange, back in zip(plan, backs):
        way, _ = ways_of(exchange)
        for place in range(back.shape[0]):
            at = index_ref[way, place]
            scratch[at] = scratch[at] + back[place].astype(F32)
    out_ref[...] = scratch[...].astype(BF16)


VMEM = pl.BlockSpec(memory_space=pltpu.VMEM)
SMEM = pl.BlockSpec(memory_space=pltpu.SMEM)


def call(kernel, ins, outs, scratch=(), flops=0, moved=0):
    return pl.pallas_call(
        kernel,
        in_specs=ins,
        out_specs=[VMEM] * len(outs),
        out_shape=outs,
        scratch_shapes=list(scratch),
        compiler_params=pltpu.CompilerParams(vmem_limit_bytes=48 * 2**20),
        cost_estimate=pl.CostEstimate(flops=flops, bytes_accessed=moved, transcendentals=0),
    )


def swapped(x, axis, bit):
    peers = lax.axis_size(axis)
    return lax.ppermute(x, axis, [(i, i ^ bit) for i in range(peers)])


def per_device(plan, node_features, weight, wigner, radial, edge_src, edge_dst, send_index, edge_count, grad_update):
    node_dev, coefs, channels = node_features.shape
    slot = send_index.shape[1]
    edges = edge_src.shape[0]
    height = -(-(node_dev + slot * len(plan)) // 16) * 16
    src, dst = edge_src.reshape(1, edges), edge_dst.reshape(1, edges)
    piece = jax.ShapeDtypeStruct((slot, coefs, channels), BF16)
    atoms = jax.ShapeDtypeStruct((node_dev, coefs, channels), BF16)
    many = jax.ShapeDtypeStruct((channels, coefs * edges), BF16)

    outgoing = call(
        functools.partial(send_kernel, plan), [SMEM, VMEM], [piece] * len(plan), moved=400000
    )(send_index, node_features)
    arrived = [lax.ppermute(x, e[0], e[5]) for x, e in zip(outgoing, plan)]

    gs, own, *backs = call(
        functools.partial(grad_kernel, plan, slot, height),
        [SMEM] + [VMEM] * 6,
        [many, jax.ShapeDtypeStruct((node_dev, coefs, channels), F32)] + [piece] * len(plan),
        [pltpu.VMEM((node_dev * ROW, channels), F32), pltpu.VMEM((height * ROW, channels), F32)],
        flops=5 * 10**9,
    )(edge_count, src, dst, radial, wigner, weight, grad_update)
    returned = [lax.ppermute(x, e[0], e[5]) for x, e in zip(backs, plan)]

    half = jax.ShapeDtypeStruct((weight.shape[0] * channels // 2, channels), F32)
    rot, keep, send = call(
        functools.partial(rot_kernel, plan, slot, height),
        [VMEM] * (4 + len(plan)),
        [many, half, jax.ShapeDtypeStruct(half.shape, BF16)],
        [pltpu.VMEM((height * ROW, channels), F32)],
        flops=5 * 10**9,
    )(src, wigner, node_features, gs, *arrived)
    total = keep + swapped(send, "shard", 1).astype(F32)
    bits = [("group", 1 << b) for b in range(lax.axis_size("group").bit_length() - 1)]
    bits += [("shard", 1 << b) for b in range(1, lax.axis_size("shard").bit_length() - 1)]
    for axis, bit in bits:
        mine = total.astype(BF16)
        total = mine.astype(F32) + swapped(mine, axis, bit).astype(F32)
    other = swapped(total, "shard", 1)
    first = lax.rem(lax.axis_index("shard"), 2) == 0
    grad_weight = jnp.concatenate(
        [jnp.where(first, total, other), jnp.where(first, other, total)], axis=0
    ).reshape(weight.shape)

    [update] = call(
        update_kernel,
        [SMEM] + [VMEM] * 5,
        [atoms],
        [pltpu.VMEM((node_dev * ROW, channels), F32)],
        flops=3 * 10**9,
    )(edge_count, dst, radial, wigner, weight, rot)
    [grad_input] = call(
        functools.partial(finish_kernel, plan),
        [SMEM] + [VMEM] * (1 + len(plan)),
        [atoms],
        [pltpu.VMEM((node_dev, coefs, channels), F32)],
        moved=800000,
    )(send_index, own, *returned)
    return update, grad_input, grad_weight


def solution(mesh):
    plan = exchanges(mesh.shape["group"], mesh.shape["shard"])
    both = ("group", "shard")
    return jax.shard_map(
        functools.partial(per_device, plan),
        mesh=mesh,
        in_specs=(
            P(both, None, None),
            P(),
            P(None, None, None, both),
            P(None, both),
            P(both),
            P(both),
            P(both, None),
            P(both),
            P(both, None, None),
        ),
        out_specs=(P(both, None, None), P(both, None, None), P()),
        check_vma=False,
    )
```

```python
import functools

import jax
import jax.numpy as jnp
from jax import lax
from jax.experimental import pallas as pl
from jax.experimental.pallas import tpu as pltpu
from jax.sharding import PartitionSpec as P

F32, BF16 = jnp.float32, jnp.bfloat16
COLS = 8
LMAX = 6
COEF = (LMAX + 1) ** 2
SIDE = 2 * LMAX + 1
ROW = 56
way_list = [(-1, -1), (-1, 0), (-1, 1), (0, -1), (0, 1), (1, -1), (1, 0), (1, 1)]


def exchanges(groups, shards):
    rows = shards // COLS
    found = []
    for dr, dc in [(0, 1), (1, -1), (1, 0), (1, 1)]:
        by = COLS * dr + dc
        for parity in (0, 1):
            pairs = []
            for s in range(shards):
                r, c = s // COLS, s % COLS
                if (r if dr else c) % 2 == parity and r + dr < rows and 0 <= c + dc < COLS:
                    pairs += [(s, s + by), (s + by, s)]
            if pairs:
                plus = way_list.index((dr, dc))
                found.append(("shard", plus, 7 - plus, "row" if dr else "col", parity, pairs))
    for parity in (0, 1):
        pairs = []
        for g in range(groups - 1):
            if g % 2 == parity:
                pairs += [(g, g + 1), (g + 1, g)]
        if pairs:
            found.append(("group", 8, 9, "group", parity, pairs))
    return found[:0:-1] + found[:1]


def ways_of(exchange):
    _, plus, minus, coordinate, parity, _ = exchange
    if coordinate == "group":
        place = lax.axis_index("group")
    elif coordinate == "row":
        place = lax.div(lax.axis_index("shard"), COLS)
    else:
        place = lax.rem(lax.axis_index("shard"), COLS)
    lower = lax.rem(place, 2) == parity
    return jnp.where(lower, plus, minus), jnp.where(lower, minus, plus)


def dot(a, b, ca, cb):
    return lax.dot_general(a, b, (((ca,), (cb,)), ((), ())), preferred_element_type=F32)


def order_coefs(order):
    found = []
    for degree in range(order, LMAX + 1):
        centre = degree * degree + degree
        found += [centre] if order == 0 else [centre - order, centre + order]
    return found


def lanes(coef, edges):
    return slice(coef * edges, (coef + 1) * edges)


def dst_hot(dst, node_dev):
    edges = dst.shape[1]
    return (lax.broadcasted_iota(jnp.int32, (node_dev, edges), 0) == dst).astype(F32).astype(BF16)


def src_hot(src, node_dev, slot, ways, height):
    edges = src.shape[1]
    row = lax.broadcasted_iota(jnp.int32, (height, edges), 0)
    code = jnp.where(row < node_dev, row, -1)
    for number, way in enumerate(ways):
        for place in range(slot):
            code = jnp.where(
                row == node_dev + slot * number + place, node_dev + slot * way + place, code
            )
    return (code == src).astype(F32).astype(BF16)


def places_of(degree, order):
    return [degree] if order == 0 else [degree - order, degree + order]


def side_by_side(pieces):
    return jnp.concatenate(pieces, axis=1)


def stage_kernel(
    plan, index_hbm, nodes_hbm, grads_hbm, wig_hbm, radial_hbm, src_hbm, dst_hbm, weight_hbm,
    nodes_ref, grads_ref, wig_ref, radial_ref, src_ref, dst_ref, weight_ref, *rest,
):
    outs, (scratch, index_ref, sems) = rest[:-3], rest[-3:]
    moves = [
        (index_hbm, index_ref), (nodes_hbm, nodes_ref), (radial_hbm, radial_ref),
        (src_hbm, src_ref), (dst_hbm, dst_ref), (wig_hbm, wig_ref), (grads_hbm, grads_ref),
        (weight_hbm, weight_ref),
    ]
    copies = [pltpu.make_async_copy(a, b, sems.at[i]) for i, (a, b) in enumerate(moves)]
    for copy in copies:
        copy.start()
    copies[0].wait()
    copies[1].wait()
    coefs, atoms, _ = nodes_ref.shape
    for coef in range(coefs):
        scratch[coef * atoms : (coef + 1) * atoms, :] = nodes_ref[coef].astype(F32)
    for exchange, out in zip(plan, outs):
        way, _ = ways_of(exchange)
        for place in range(out.shape[0]):
            at = index_ref[place, way]
            out[place] = scratch[pl.ds(at, coefs, stride=atoms), :].astype(BF16)
    for copy in copies[2:]:
        copy.wait()


def expand_kernel(
    plan, slot, height, count_ref, src_ref, dst_ref, radial_ref, wig_ref, grad_ref,
    gain_ref, gr_ref, gs_ref, *rest,
):
    to_src, to_dst, wide = rest[: LMAX + 1], rest[LMAX + 1 : -1], rest[-1]
    node_dev = grad_ref.shape[1]
    edges = wig_ref.shape[3]
    radial = radial_ref[...]
    at = lax.broadcasted_iota(jnp.int32, radial.shape, 1)
    gain = jnp.where(at < count_ref[0], radial, 0.0)
    gain_ref[...] = gain
    dst = dst_hot(dst_ref[...], node_dev)
    src = src_hot(src_ref[...], node_dev, slot, [ways_of(x)[1] for x in plan], height)
    for i in range(SIDE):
        for j in range(SIDE):
            start = (i * SIDE + j) * 8
            wide[start : start + LMAX + 1, :] = wig_ref[i, j].astype(F32)
    for degree in range(LMAX, -1, -1):
        width = 2 * degree + 1
        base = degree * degree
        for i in range(width):
            for j in range(width):
                at = (i * SIDE + j) * 8 + degree
                row = jnp.broadcast_to(wide[at : at + 1, :], (16, edges)).astype(BF16)
                for start in range(0, node_dev, 16):
                    low = j * node_dev + start
                    to_dst[degree][low : low + 16, lanes(i, edges)] = dst[start : start + 16] * row
                for start in range(0, height, 16):
                    low = j * height + start
                    to_src[degree][low : low + 16, lanes(i, edges)] = src[start : start + 16] * row
        atoms = jnp.concatenate([grad_ref[base + j] for j in range(width)], axis=0)
        gr = dot(atoms, to_dst[degree][...], 0, 0).astype(BF16)
        gr_ref[:, base * edges : (base + width) * edges] = gr
        for i in range(width):
            scale = gain[abs(i - degree) : abs(i - degree) + 1]
            gs_ref[:, lanes(base + i, edges)] = (gr[:, lanes(i, edges)].astype(F32) * scale).astype(BF16)


def rot_kernel(slot, height, nodes_ref, gs_ref, *rest):
    to_src, halos = rest[: LMAX + 1], rest[LMAX + 1 : -4]
    rot_ref, keep_ref, send_ref, scratch = rest[-4:]
    node_dev = nodes_ref.shape[1]
    more = height - node_dev
    edges = rot_ref.shape[1] // COEF
    scratch[slot * len(halos) * ROW :, :] = jnp.zeros(
        ((more - slot * len(halos)) * ROW, scratch.shape[1]), F32
    )
    for number, halo in enumerate(halos):
        for place in range(slot):
            start = (slot * number + place) * ROW
            scratch[start : start + COEF, :] = halo[place].astype(F32)
    for degree in range(LMAX, -1, -1):
        base, end = degree * degree, (degree + 1) * (degree + 1)
        pieces = []
        for coef in range(base, end):
            pieces += [nodes_ref[coef], scratch[pl.ds(coef, more, stride=ROW), :].astype(BF16)]
        rot = dot(jnp.concatenate(pieces, axis=0), to_src[degree][...], 0, 0).astype(BF16)
        rot_ref[:, base * edges : end * edges] = rot
    parts = []
    for order in range(LMAX + 1):
        coefs = order_coefs(order)
        left = side_by_side([rot_ref[:, lanes(k, edges)] for k in coefs])
        right = side_by_side([gs_ref[:, lanes(k, edges)] for k in coefs])
        parts.append(dot(left, right, 1, 1))
    whole = jnp.concatenate(parts, axis=0)
    half = whole.shape[0] // 2
    first = lax.rem(lax.axis_index("shard"), 2) == 0
    keep_ref[...] = jnp.where(first, whole[:half], whole[half:])
    send_ref[...] = jnp.where(first, whole[half:], whole[:half]).astype(BF16)


def mixed(values_ref, weight_ref, gain, degree, forward, edges):
    base = degree * degree
    found = [None] * (2 * degree + 1)
    for order in range(degree + 1):
        places = places_of(degree, order)
        part = side_by_side([values_ref[:, lanes(base + i, edges)] for i in places])
        scale = side_by_side([gain[order : order + 1]] * len(places))
        out = (dot(weight_ref[order], part, 0 if forward else 1, 0) * scale).astype(BF16)
        for number, i in enumerate(places):
            found[i] = out[:, lanes(number, edges)]
    return side_by_side(found)


def back_kernel(slot, height, gain_ref, weight_ref, gr_ref, *rest):
    to_src, own_ref, backs, scratch = rest[: LMAX + 1], rest[LMAX + 1], rest[LMAX + 2 : -1], rest[-1]
    node_dev = own_ref.shape[0] // COEF
    more = height - node_dev
    edges = gr_ref.shape[1] // COEF
    gain = gain_ref[...]
    for degree in range(LMAX, -1, -1):
        base = degree * degree
        back = mixed(gr_ref, weight_ref, gain, degree, False, edges)
        out = dot(to_src[degree][...], back, 1, 1)
        for j in range(2 * degree + 1):
            coef, low = base + j, j * height
            own_ref[coef * node_dev : (coef + 1) * node_dev, :] = out[low : low + node_dev]
            scratch[pl.ds(coef, more, stride=ROW), :] = out[low + node_dev : low + height]
    for number, back_ref in enumerate(backs):
        for place in range(slot):
            start = (slot * number + place) * ROW
            back_ref[place] = scratch[start : start + COEF, :].astype(BF16)


def update_kernel(gain_ref, weight_ref, rot_ref, *rest):
    to_dst, out_ref = rest[:-1], rest[-1]
    node_dev = out_ref.shape[1]
    edges = rot_ref.shape[1] // COEF
    gain = gain_ref[...]
    for degree in range(LMAX, -1, -1):
        msg = mixed(rot_ref, weight_ref, gain, degree, True, edges)
        out = dot(to_dst[degree][...], msg, 1, 1).astype(BF16)
        for j in range(2 * degree + 1):
            out_ref[degree * degree + j] = out[j * node_dev : (j + 1) * node_dev]


def finish_kernel(plan, index_ref, own_ref, *rest):
    backs, out_ref, scratch = rest[:-2], rest[-2], rest[-1]
    coefs, atoms, _ = out_ref.shape
    scratch[...] = own_ref[...]
    for exchange, back in zip(plan, backs):
        way, _ = ways_of(exchange)
        for place in range(back.shape[0]):
            at = index_ref[place, way]
            rows = scratch[pl.ds(at, coefs, stride=atoms), :]
            scratch[pl.ds(at, coefs, stride=atoms), :] = rows + back[place].astype(F32)
    for coef in range(coefs):
        out_ref[coef] = scratch[coef * atoms : (coef + 1) * atoms, :].astype(BF16)


def join_kernel(mine_ref, other_ref, out_ref):
    half = mine_ref.shape[0]
    first = lax.rem(lax.axis_index("shard"), 2) == 0
    mine, other = mine_ref[...], other_ref[...]
    out_ref[:half, :] = jnp.where(first, mine, other)
    out_ref[half:, :] = jnp.where(first, other, mine)


VMEM = pl.BlockSpec(memory_space=pltpu.VMEM)
SMEM = pl.BlockSpec(memory_space=pltpu.SMEM)
HBM = pl.BlockSpec(memory_space=pltpu.HBM)


def call(kernel, ins, outs, scratch=(), flops=0, moved=0, vmem=32):
    return pl.pallas_call(
        kernel,
        in_specs=ins,
        out_specs=[VMEM] * len(outs),
        out_shape=outs,
        scratch_shapes=list(scratch),
        compiler_params=pltpu.CompilerParams(vmem_limit_bytes=vmem * 2**20),
        cost_estimate=pl.CostEstimate(flops=flops, bytes_accessed=moved, transcendentals=0),
    )


def total_of(keep, send, fills):
    groups, shards = lax.axis_size("group"), lax.axis_size("shard")
    both = ("group", "shard")
    bits = [("group", 1 << b) for b in range(groups.bit_length() - 1)]
    bits += [("shard", 1 << b) for b in range(1, shards.bit_length() - 1)]
    turn = len(bits) // 2
    pairs = [(s, s ^ 1) for s in range(shards)]
    total = keep + lax.ppermute(send, "shard", pairs).astype(F32)
    for step in range(len(bits)):
        pairs = []
        for g in range(groups):
            for s in range(shards):
                axis, bit = bits[(step + turn * (s % 2)) % len(bits)]
                to = (g ^ bit) * shards + s if axis == "group" else g * shards + (s ^ bit)
                pairs.append((g * shards + s, to))
        mine = total.astype(BF16)
        theirs = lax.ppermute(mine, both, pairs)
        if step < len(fills):
            theirs = fills[step](mine, theirs)
        total = mine.astype(F32) + theirs.astype(F32)
    return total


def per_device(plan, node_features, weight, wigner, radial, edge_src, edge_dst, send_index, edge_count, grad_update):
    node_dev, coefs, channels = node_features.shape
    slot = send_index.shape[1]
    edges = edge_src.shape[0]
    height = node_dev + -(-(slot * len(plan)) // 16) * 16
    src, dst = edge_src.reshape(1, edges), edge_dst.reshape(1, edges)
    nodes = node_features.transpose(1, 0, 2)
    grads = grad_update.transpose(1, 0, 2)
    wig = wigner.transpose(1, 2, 0, 3)
    index = send_index.T
    shape = jax.ShapeDtypeStruct
    piece = shape((slot, coefs, channels), BF16)
    atoms = shape((coefs, node_dev, channels), BF16)
    many = shape((channels, coefs * edges), BF16)
    wide = pltpu.VMEM((coefs * node_dev, channels), F32)

    nodes, grads, wig, radials, src, dst, weights, *outgoing = call(
        functools.partial(stage_kernel, plan),
        [HBM] * 8,
        [shape(x.shape, x.dtype) for x in (nodes, grads, wig, radial, src, dst, weight)] + [piece] * len(plan),
        [
            wide,
            pltpu.SMEM(index.shape, jnp.int32),
            pltpu.SemaphoreType.DMA((8,)),
        ],
        moved=400000,
        vmem=32,
    )(
        *[pltpu.with_memory_space_constraint(x, pltpu.HBM) for x in (index, nodes, grads, wig, radial, src, dst, weight)],
    )
    arrived = [lax.ppermute(x, e[0], e[5]) for x, e in zip(outgoing, plan)]

    widths = [2 * degree + 1 for degree in range(LMAX + 1)]
    gain, gr, gs, *matrices = call(
        functools.partial(expand_kernel, plan, slot, height),
        [SMEM] + [VMEM] * 5,
        [shape(radial.shape, F32), many, many]
        + [shape((width * height, width * edges), BF16) for width in widths]
        + [shape((width * node_dev, width * edges), BF16) for width in widths],
        [pltpu.VMEM((SIDE * SIDE * 8, edges), F32)],
        flops=3 * 10**9,
    )(edge_count, src, dst, radials, wig, grads)
    to_src, to_dst = matrices[: LMAX + 1], matrices[LMAX + 1 :]

    half = shape((weight.shape[0] * channels // 2, channels), F32)
    rot, keep, send = call(
        functools.partial(rot_kernel, slot, height),
        [VMEM] * (2 + LMAX + 1 + len(plan)),
        [many, half, shape(half.shape, BF16)],
        [pltpu.VMEM(((height - node_dev) * ROW, channels), F32)],
        flops=3 * 10**9,
    )(nodes, gs, *to_src, *arrived)

    held = {}

    def run_back(mine, theirs):
        mine, late = lax.optimization_barrier((mine, gr))
        out = call(
            functools.partial(back_kernel, slot, height),
            [VMEM] * (3 + LMAX + 1),
            [shape((coefs * node_dev, channels), F32)] + [piece] * len(plan),
            [pltpu.VMEM(((height - node_dev) * ROW, channels), F32)],
            flops=3 * 10**9,
        )(gain, weights, late, *to_src)
        theirs, *out = lax.optimization_barrier((theirs, *out))
        held["own"], held["backs"] = out[0], out[1:]
        return theirs

    def run_update(mine, theirs):
        mine, late = lax.optimization_barrier((mine, rot))
        [out] = call(
            update_kernel, [VMEM] * (3 + LMAX + 1), [atoms], flops=3 * 10**9
        )(gain, weights, late, *to_dst)
        theirs, held["update"] = lax.optimization_barrier((theirs, out))
        return theirs

    returned = [None] * len(plan)

    def run_returns(numbers):
        def run(mine, theirs):
            mine, *late = lax.optimization_barrier((mine, *[held["backs"][i] for i in numbers]))
            for i, x in zip(numbers, late):
                returned[i] = lax.ppermute(x, plan[i][0], plan[i][5])
            return theirs

        return run

    def end_returns(numbers, more):
        def run(mine, theirs):
            theirs, *came = lax.optimization_barrier((theirs, *[returned[i] for i in numbers]))
            for i, x in zip(numbers, came):
                returned[i] = x
            return more(mine, theirs)

        return run

    cut = len(plan) // 2
    low, high = range(cut), range(cut, len(plan))
    fills = [run_back, run_returns(low), end_returns(low, run_returns(high)), end_returns(high, run_update)]
    total = total_of(keep, send, fills)
    other = lax.ppermute(total, "shard", [(s, s ^ 1) for s in range(lax.axis_size("shard"))])
    [grad_weight] = call(
        join_kernel, [VMEM] * 2, [shape((2 * half.shape[0], channels), F32)], moved=10**6
    )(total, other)
    [grad_input] = call(
        functools.partial(finish_kernel, plan), [SMEM] + [VMEM] * (1 + len(plan)), [atoms], [wide], moved=800000
    )(index, held["own"], *returned)
    return (
        held["update"].transpose(1, 0, 2),
        grad_input.transpose(1, 0, 2),
        grad_weight.reshape(weight.shape),
    )


def solution(mesh):
    plan = exchanges(mesh.shape["group"], mesh.shape["shard"])
    both = ("group", "shard")
    return jax.shard_map(
        functools.partial(per_device, plan),
        mesh=mesh,
        in_specs=(
            P(both, None, None),
            P(),
            P(None, None, None, both),
            P(None, both),
            P(both),
            P(both),
            P(both, None),
            P(both),
            P(both, None, None),
        ),
        out_specs=(P(both, None, None), P(both, None, None), P()),
        check_vma=False,
    )
```

```python
import functools

import jax
import jax.numpy as jnp
from jax import lax
from jax.experimental import pallas as pl
from jax.experimental.pallas import tpu as pltpu
from jax.sharding import PartitionSpec as P

F32, BF16 = jnp.float32, jnp.bfloat16
COLS = 8
LMAX = 6
COEF = (LMAX + 1) ** 2
SIDE = 2 * LMAX + 1
ROW = 56
way_list = [(-1, -1), (-1, 0), (-1, 1), (0, -1), (0, 1), (1, -1), (1, 0), (1, 1)]


def exchanges(groups, shards):
    rows = shards // COLS
    found = []
    for dr, dc in [(0, 1), (1, -1), (1, 0), (1, 1)]:
        by = COLS * dr + dc
        for parity in (0, 1):
            pairs = []
            for s in range(shards):
                r, c = s // COLS, s % COLS
                if (r if dr else c) % 2 == parity and r + dr < rows and 0 <= c + dc < COLS:
                    pairs += [(s, s + by), (s + by, s)]
            if pairs:
                plus = way_list.index((dr, dc))
                found.append(("shard", plus, 7 - plus, "row" if dr else "col", parity, pairs))
    found.sort(key=lambda e: e[5][0][1] - e[5][0][0] == 1 and e[4] == 0)
    if groups != 4:
        raise ValueError("for 4 groups")
    return [("group", 8, 9, "group", parity, None) for parity in (0, 1)] + found


def relay(x):
    one = swapped(x, "group", 1)
    return one, lambda: swapped(one, "group", 2)


def swapped(x, axis, bit):
    return lax.ppermute(x, axis, [(i, i ^ bit) for i in range(lax.axis_size(axis))])


def ways_of(exchange):
    _, plus, minus, coordinate, parity, _ = exchange
    if coordinate == "group":
        place = lax.axis_index("group")
    elif coordinate == "row":
        place = lax.div(lax.axis_index("shard"), COLS)
    else:
        place = lax.rem(lax.axis_index("shard"), COLS)
    lower = lax.rem(place, 2) == parity
    return jnp.where(lower, plus, minus), jnp.where(lower, minus, plus)


def dot(a, b, ca, cb):
    return lax.dot_general(a, b, (((ca,), (cb,)), ((), ())), preferred_element_type=F32)


def order_coefs(order):
    found = []
    for degree in range(order, LMAX + 1):
        centre = degree * degree + degree
        found += [centre] if order == 0 else [centre - order, centre + order]
    return found


def lanes(coef, edges):
    return slice(coef * edges, (coef + 1) * edges)


def dst_hot(dst, node_dev):
    edges = dst.shape[1]
    return (lax.broadcasted_iota(jnp.int32, (node_dev, edges), 0) == dst).astype(F32).astype(BF16)


def src_hot(src, node_dev, slot, ways, height):
    edges = src.shape[1]
    row = lax.broadcasted_iota(jnp.int32, (height, edges), 0)
    code = jnp.where(row < node_dev, row, -1)
    for number, way in enumerate(ways):
        for place in range(slot):
            code = jnp.where(
                row == node_dev + slot * number + place, node_dev + slot * way + place, code
            )
    return (code == src).astype(F32).astype(BF16)


def places_of(degree, order):
    return [degree] if order == 0 else [degree - order, degree + order]


def side_by_side(pieces):
    return jnp.concatenate(pieces, axis=1)


def stage_kernel(
    plan, index_hbm, nodes_hbm, grads_hbm, wig_hbm, radial_hbm, src_hbm, dst_hbm, weight_hbm,
    nodes_ref, grads_ref, wig_ref, radial_ref, src_ref, dst_ref, weight_ref, *rest,
):
    outs, (scratch, index_ref, sems) = rest[:-3], rest[-3:]
    moves = [
        (index_hbm, index_ref), (nodes_hbm, nodes_ref), (radial_hbm, radial_ref),
        (src_hbm, src_ref), (dst_hbm, dst_ref), (wig_hbm, wig_ref), (grads_hbm, grads_ref),
        (weight_hbm, weight_ref),
    ]
    copies = [pltpu.make_async_copy(a, b, sems.at[i]) for i, (a, b) in enumerate(moves)]
    for copy in copies:
        copy.start()
    copies[0].wait()
    copies[1].wait()
    coefs, atoms, _ = nodes_ref.shape
    scratch[coefs * atoms :, :] = jnp.zeros((scratch.shape[0] - coefs * atoms, scratch.shape[1]), F32)
    for coef in range(coefs):
        scratch[coef * atoms : (coef + 1) * atoms, :] = nodes_ref[coef].astype(F32)
    slot = index_ref.shape[0]
    for number, exchange in enumerate(plan):
        way, _ = ways_of(exchange)
        out, base = (outs[0], slot * number) if number < 2 else (outs[number - 1], 0)
        for place in range(slot):
            at = index_ref[place, way]
            out[base + place] = scratch[pl.ds(at, coefs, stride=atoms), :].astype(BF16)
    for copy in copies[2:]:
        copy.wait()


def expand_kernel(
    plan, slot, height, src_ref, dst_ref, wig_ref, grad_ref, nodes_ref, gr_ref, own_ref, *rest,
):
    to_own, to_halo, to_dst, wide = (*(rest[k * (LMAX + 1) : (k + 1) * (LMAX + 1)] for k in range(3)), rest[-1])
    node_dev = grad_ref.shape[1]
    edges = wig_ref.shape[3]
    dst = dst_hot(dst_ref[...], node_dev)
    src = src_hot(src_ref[...], node_dev, slot, [ways_of(x)[1] for x in plan], height)
    hots = [(to_own, src[:node_dev]), (to_halo, src[node_dev:]), (to_dst, dst)]
    for i in range(SIDE):
        for j in range(SIDE):
            start = (i * SIDE + j) * 8
            wide[start : start + LMAX + 1, :] = wig_ref[i, j].astype(F32)
    for degree in range(LMAX, -1, -1):
        width = 2 * degree + 1
        base = degree * degree
        for i in range(width):
            for j in range(width):
                at = (i * SIDE + j) * 8 + degree
                row = jnp.broadcast_to(wide[at : at + 1, :], (16, edges)).astype(BF16)
                for refs, hot in hots:
                    tall = hot.shape[0]
                    for start in range(0, tall, 16):
                        low = j * tall + start
                        refs[degree][low : low + 16, lanes(i, edges)] = hot[start : start + 16] * row
        atoms = jnp.concatenate([grad_ref[base + j] for j in range(width)], axis=0)
        gr = dot(atoms, to_dst[degree][...], 0, 0).astype(BF16)
        gr_ref[:, base * edges : (base + width) * edges] = gr
        atoms = jnp.concatenate([nodes_ref[base + j] for j in range(width)], axis=0)
        own = dot(atoms, to_own[degree][...], 0, 0).astype(BF16)
        own_ref[:, base * edges : (base + width) * edges] = own


def rot_kernel(slot, count_ref, radial_ref, gr_ref, own_ref, *rest):
    to_halo, (one, two, *more_halos) = rest[: LMAX + 1], rest[LMAX + 1 : -5]
    halos = [one.at[:slot], two.at[slot:], *more_halos]
    gain_ref, rot_ref, keep_ref, send_ref, scratch = rest[-5:]
    radial = radial_ref[...]
    at = lax.broadcasted_iota(jnp.int32, radial.shape, 1)
    gain = jnp.where(at < count_ref[0], radial, 0.0)
    gain_ref[...] = gain
    tall = scratch.shape[0] // ROW
    edges = rot_ref.shape[1] // COEF
    scratch[slot * len(halos) * ROW :, :] = jnp.zeros(
        ((tall - slot * len(halos)) * ROW, scratch.shape[1]), F32
    )
    for number, halo in enumerate(halos):
        for place in range(slot):
            start = (slot * number + place) * ROW
            scratch[start : start + COEF, :] = halo[place].astype(F32)
    for degree in range(LMAX, -1, -1):
        base, end = degree * degree, (degree + 1) * (degree + 1)
        span = slice(base * edges, end * edges)
        pieces = [scratch[pl.ds(coef, tall, stride=ROW), :].astype(BF16) for coef in range(base, end)]
        rot = dot(jnp.concatenate(pieces, axis=0), to_halo[degree][...], 0, 0).astype(BF16)
        rot_ref[:, span] = own_ref[:, span] + rot
    parts = []
    for order in range(LMAX + 1):
        coefs = order_coefs(order)
        left = side_by_side([rot_ref[:, lanes(k, edges)] for k in coefs])
        scale = gain[order : order + 1]
        right = side_by_side([(gr_ref[:, lanes(k, edges)].astype(F32) * scale).astype(BF16) for k in coefs])
        parts.append(dot(left, right, 1, 1))
    whole = jnp.concatenate(parts, axis=0)
    half = whole.shape[0] // 2
    first = lax.rem(lax.axis_index("shard"), 2) == 0
    keep_ref[...] = jnp.where(first, whole[:half], whole[half:])
    send_ref[...] = jnp.where(first, whole[half:], whole[:half]).astype(BF16)


def mixed(values_ref, weight_ref, gain, degree, forward, edges):
    base = degree * degree
    found = [None] * (2 * degree + 1)
    for order in range(degree + 1):
        places = places_of(degree, order)
        part = side_by_side([values_ref[:, lanes(base + i, edges)] for i in places])
        scale = side_by_side([gain[order : order + 1]] * len(places))
        out = (dot(weight_ref[order], part, 0 if forward else 1, 0) * scale).astype(BF16)
        for number, i in enumerate(places):
            found[i] = out[:, lanes(number, edges)]
    return side_by_side(found)


def back_kernel(gain_ref, weight_ref, gr_ref, *rest):
    to_own, to_halo, rest = rest[: LMAX + 1], rest[LMAX + 1 : 2 * LMAX + 2], rest[2 * LMAX + 2 :]
    own_ref, backs, scratch = rest[0], rest[1:-1], rest[-1]
    node_dev, tall = own_ref.shape[0] // COEF, scratch.shape[0] // ROW
    edges = gr_ref.shape[1] // COEF
    gain = gain_ref[...]
    scratch[...] = jnp.zeros(scratch.shape, F32)
    for degree in range(LMAX, -1, -1):
        base, width = degree * degree, 2 * degree + 1
        back = mixed(gr_ref, weight_ref, gain, degree, False, edges)
        out = dot(jnp.concatenate([to_own[degree][...], to_halo[degree][...]], axis=0), back, 1, 1)
        own_ref[base * node_dev : (base + width) * node_dev, :] = out[: width * node_dev]
        for j in range(width):
            low = width * node_dev + j * tall
            scratch[pl.ds(base + j, tall, stride=ROW), :] = out[low : low + tall]
    start = 0
    for back_ref in backs:
        back_ref[...] = scratch[start : start + back_ref.shape[0], :].astype(BF16)
        start += back_ref.shape[0]


def update_kernel(gain_ref, weight_ref, rot_ref, *rest):
    to_dst, out_ref = rest[:-1], rest[-1]
    node_dev = out_ref.shape[1]
    edges = rot_ref.shape[1] // COEF
    gain = gain_ref[...]
    for degree in range(LMAX, -1, -1):
        msg = mixed(rot_ref, weight_ref, gain, degree, True, edges)
        out = dot(to_dst[degree][...], msg, 1, 1).astype(BF16)
        for j in range(2 * degree + 1):
            out_ref[degree * degree + j] = out[j * node_dev : (j + 1) * node_dev]


def step_kernel(mine_ref, theirs_ref, out_ref):
    out_ref[...] = (mine_ref[...].astype(F32) + theirs_ref[...].astype(F32)).astype(BF16)


def finish_kernel(plan, slot, index_ref, own_ref, *rest):
    (one, two, *backs), out_ref, scratch = rest[:-2], rest[-2], rest[-1]
    coefs, atoms, _ = out_ref.shape
    backs = [one.at[: slot * ROW], two.at[slot * ROW :], *backs]
    scratch[: coefs * atoms, :] = own_ref[...]
    for exchange, back in zip(plan, backs):
        way, _ = ways_of(exchange)
        for place in range(slot):
            at = index_ref[place, way]
            rows = scratch[pl.ds(at, coefs, stride=atoms), :]
            come = back[place * ROW : place * ROW + coefs, :].astype(F32)
            scratch[pl.ds(at, coefs, stride=atoms), :] = rows + come
    for coef in range(coefs):
        out_ref[coef] = scratch[coef * atoms : (coef + 1) * atoms, :].astype(BF16)


def join_kernel(mine_ref, other_ref, out_ref):
    half = mine_ref.shape[0]
    first = lax.rem(lax.axis_index("shard"), 2) == 0
    mine, other = mine_ref[...], other_ref[...]
    out_ref[:half, :] = jnp.where(first, mine, other)
    out_ref[half:, :] = jnp.where(first, other, mine)


VMEM = pl.BlockSpec(memory_space=pltpu.VMEM)
SMEM = pl.BlockSpec(memory_space=pltpu.SMEM)
HBM = pl.BlockSpec(memory_space=pltpu.HBM)


def call(kernel, ins, outs, scratch=(), flops=0, moved=0, vmem=32):
    return pl.pallas_call(
        kernel,
        in_specs=ins,
        out_specs=[VMEM] * len(outs),
        out_shape=outs,
        scratch_shapes=list(scratch),
        compiler_params=pltpu.CompilerParams(vmem_limit_bytes=vmem * 2**20),
        cost_estimate=pl.CostEstimate(flops=flops, bytes_accessed=moved, transcendentals=0),
    )


def total_of(keep, send, fills):
    groups, shards = lax.axis_size("group"), lax.axis_size("shard")
    both = ("group", "shard")
    along = [("shard", 1 << b) for b in range(1, shards.bit_length() - 1)]
    within = [("group", 1 << b) for b in range(groups.bit_length() - 1)]
    orders = [within + along, along + within]
    total = keep + lax.ppermute(send, "shard", [(s, s ^ 1) for s in range(shards)]).astype(F32)
    mine = total.astype(BF16)
    for step in range(len(orders[0])):
        if step:
            [mine] = call(step_kernel, [VMEM] * 2, [jax.ShapeDtypeStruct(mine.shape, BF16)], moved=350000)(mine, came)
        pairs = []
        for g in range(groups):
            for s in range(shards):
                axis, bit = orders[s % 2][step]
                to = (g ^ bit) * shards + s if axis == "group" else g * shards + (s ^ bit)
                pairs.append((g * shards + s, to))
        came = lax.ppermute(mine, both, pairs)
        for fill in fills.get(step, []):
            came = fill(mine, came)
    return mine.astype(F32) + came.astype(F32)


def per_device(plan, node_features, weight, wigner, radial, edge_src, edge_dst, send_index, edge_count, grad_update):
    node_dev, coefs, channels = node_features.shape
    slot = send_index.shape[1]
    edges = edge_src.shape[0]
    tall = -(-(slot * len(plan)) // 16) * 16
    height = node_dev + tall
    src, dst = edge_src.reshape(1, edges), edge_dst.reshape(1, edges)
    nodes = node_features.transpose(1, 0, 2)
    grads = grad_update.transpose(1, 0, 2)
    wig = wigner.transpose(1, 2, 0, 3)
    index = send_index.T
    shape = jax.ShapeDtypeStruct
    piece, pair = (shape((n * slot, coefs, channels), BF16) for n in (1, 2))
    atoms = shape((coefs, node_dev, channels), BF16)
    many = shape((channels, coefs * edges), BF16)
    wide = pltpu.VMEM((ROW * node_dev, channels), F32)

    inner = plan[2:]
    nodes, grads, wig, radials, src, dst, weights, *outgoing = call(
        functools.partial(stage_kernel, plan),
        [HBM] * 8,
        [shape(x.shape, x.dtype) for x in (nodes, grads, wig, radial, src, dst, weight)]
        + [pair] + [piece] * len(inner),
        [
            wide,
            pltpu.SMEM(index.shape, jnp.int32),
            pltpu.SemaphoreType.DMA((8,)),
        ],
        moved=400000,
        vmem=32,
    )(
        *[pltpu.with_memory_space_constraint(x, pltpu.HBM) for x in (index, nodes, grads, wig, radial, src, dst, weight)],
    )
    one, two = relay(outgoing[0])
    arrived = [lax.ppermute(x, e[0], e[5]) for x, e in zip(outgoing[1:], inner)]
    arrived = [one, two(), *arrived]

    widths = [2 * degree + 1 for degree in range(LMAX + 1)]
    gr, own_rot, *matrices = call(
        functools.partial(expand_kernel, plan, slot, height),
        [VMEM] * 5,
        [many, many]
        + [shape((width * n, width * edges), BF16) for n in (node_dev, tall, node_dev) for width in widths],
        [pltpu.VMEM((SIDE * SIDE * 8, edges), F32)],
        flops=3 * 10**9,
    )(src, dst, wig, grads, nodes)
    to_own, to_halo, to_dst = (matrices[k * (LMAX + 1) : (k + 1) * (LMAX + 1)] for k in range(3))

    half = shape((weight.shape[0] * channels // 2, channels), F32)
    gain, rot, keep, send = call(
        functools.partial(rot_kernel, slot),
        [SMEM] + [VMEM] * (3 + LMAX + 1 + len(plan)),
        [shape(radial.shape, F32), many, half, shape(half.shape, BF16)],
        [pltpu.VMEM((tall * ROW, channels), F32)],
        flops=3 * 10**9,
    )(edge_count, radials, gr, own_rot, *to_halo, *arrived)

    held = {}

    def run_back(mine, theirs):
        mine, late = lax.optimization_barrier((mine, gr))
        out = call(
            back_kernel,
            [VMEM] * (3 + 2 * (LMAX + 1)),
            [shape((coefs * node_dev, channels), F32), shape((2 * slot * ROW, channels), BF16)]
            + [shape((slot * ROW, channels), BF16)] * len(inner),
            [pltpu.VMEM((tall * ROW, channels), F32)],
            flops=3 * 10**9,
        )(gain, weights, late, *to_own, *to_halo)
        theirs, *out = lax.optimization_barrier((theirs, *out))
        held["own"], held["backs"] = out[0], out[1:]
        return theirs

    def run_update(mine, theirs):
        mine, late = lax.optimization_barrier((mine, rot))
        [out] = call(
            update_kernel, [VMEM] * (3 + LMAX + 1), [atoms], flops=3 * 10**9
        )(gain, weights, late, *to_dst)
        theirs, held["update"] = lax.optimization_barrier((theirs, out))
        return theirs

    returned = {}

    def go(number, x):
        if number < 2:
            return swapped(x, "group", 1 << number)
        return lax.ppermute(x, plan[number][0], plan[number][5])

    def run_returns(numbers):
        def run(mine, theirs):
            ready = [returned[0] if i == 1 else held["backs"][max(i - 1, 0)] for i in numbers]
            mine, *late = lax.optimization_barrier((mine, *ready))
            for i, x in zip(numbers, late):
                returned[i] = go(i, x)
            return theirs

        return run

    def end_returns(numbers):
        def run(mine, theirs):
            theirs, *came = lax.optimization_barrier((theirs, *[returned[i] for i in numbers]))
            for i, x in zip(numbers, came):
                returned[i] = x
            return theirs

        return run

    whole = range(len(plan))
    fills = {0: [run_back], 1: [run_returns(whole[2:]), run_returns([0]), end_returns([0])], 2: [run_returns([1]), end_returns(whole[2:])], 3: [end_returns([1]), run_update]}
    total = total_of(keep, send, fills)
    other = lax.ppermute(total, "shard", [(s, s ^ 1) for s in range(lax.axis_size("shard"))])
    [grad_weight] = call(
        join_kernel, [VMEM] * 2, [shape((2 * half.shape[0], channels), F32)], moved=10**6
    )(total, other)
    [grad_input] = call(
        functools.partial(finish_kernel, plan, slot),
        [SMEM] + [VMEM] * (1 + len(plan)),
        [atoms],
        [wide],
        moved=800000,
    )(index, held["own"], *[returned[i] for i in whole])
    return (
        held["update"].transpose(1, 0, 2),
        grad_input.transpose(1, 0, 2),
        grad_weight.reshape(weight.shape),
    )


def solution(mesh):
    plan = exchanges(mesh.shape["group"], mesh.shape["shard"])
    both = ("group", "shard")
    return jax.shard_map(
        functools.partial(per_device, plan),
        mesh=mesh,
        in_specs=(
            P(both, None, None),
            P(),
            P(None, None, None, both),
            P(None, both),
            P(both),
            P(both),
            P(both, None),
            P(both),
            P(both, None, None),
        ),
        out_specs=(P(both, None, None), P(both, None, None), P()),
        check_vma=False,
    )
```

```python
import functools

import jax
import jax.numpy as jnp
from jax import lax
from jax.experimental import pallas as pl
from jax.experimental.pallas import tpu as pltpu
from jax.sharding import PartitionSpec as P

F32, BF16 = jnp.float32, jnp.bfloat16
COLS = 8
LMAX = 6
COEF = (LMAX + 1) ** 2
SIDE = 2 * LMAX + 1
ROW = 56
way_list = [(-1, -1), (-1, 0), (-1, 1), (0, -1), (0, 1), (1, -1), (1, 0), (1, 1)]


def exchanges(groups, shards):
    rows = shards // COLS
    found = []
    for dr, dc in [(0, 1), (1, -1), (1, 0), (1, 1)]:
        by = COLS * dr + dc
        for parity in (0, 1):
            pairs = []
            for s in range(shards):
                r, c = s // COLS, s % COLS
                if (r if dr else c) % 2 == parity and r + dr < rows and 0 <= c + dc < COLS:
                    pairs += [(s, s + by), (s + by, s)]
            if pairs:
                plus = way_list.index((dr, dc))
                found.append(("shard", plus, 7 - plus, "row" if dr else "col", parity, pairs))
    found.sort(key=lambda e: e[5][0][1] - e[5][0][0] == 1 and e[4] == 0)
    if groups != 4:
        raise ValueError("for 4 groups")
    return [("group", 8, 9, "group", parity, None) for parity in (0, 1)] + found


def relay(x):
    one = swapped(x, "group", 1)
    return one, lambda: swapped(one[one.shape[0] // 2 :], "group", 2)


def swapped(x, axis, bit):
    return lax.ppermute(x, axis, [(i, i ^ bit) for i in range(lax.axis_size(axis))])


def ways_of(exchange):
    _, plus, minus, coordinate, parity, _ = exchange
    if coordinate == "group":
        place = lax.axis_index("group")
    elif coordinate == "row":
        place = lax.div(lax.axis_index("shard"), COLS)
    else:
        place = lax.rem(lax.axis_index("shard"), COLS)
    lower = lax.rem(place, 2) == parity
    return jnp.where(lower, plus, minus), jnp.where(lower, minus, plus)


def dot(a, b, ca, cb):
    return lax.dot_general(a, b, (((ca,), (cb,)), ((), ())), preferred_element_type=F32)


def order_coefs(order):
    found = []
    for degree in range(order, LMAX + 1):
        centre = degree * degree + degree
        found += [centre] if order == 0 else [centre - order, centre + order]
    return found


def lanes(coef, edges):
    return slice(coef * edges, (coef + 1) * edges)


def dst_hot(dst, node_dev):
    edges = dst.shape[1]
    return (lax.broadcasted_iota(jnp.int32, (node_dev, edges), 0) == dst).astype(F32).astype(BF16)


def src_hot(src, node_dev, slot, ways, height):
    edges = src.shape[1]
    row = lax.broadcasted_iota(jnp.int32, (height, edges), 0)
    code = jnp.where(row < node_dev, row, -1)
    for number, way in enumerate(ways):
        for place in range(slot):
            code = jnp.where(
                row == node_dev + slot * number + place, node_dev + slot * way + place, code
            )
    return (code == src).astype(F32).astype(BF16)


def places_of(degree, order):
    return [degree] if order == 0 else [degree - order, degree + order]


def side_by_side(pieces):
    return jnp.concatenate(pieces, axis=1)


def stage_kernel(
    plan, index_hbm, nodes_hbm, grads_hbm, wig_hbm, radial_hbm, src_hbm, dst_hbm, weight_hbm,
    nodes_ref, grads_ref, wig_ref, radial_ref, src_ref, dst_ref, weight_ref, *rest,
):
    outs, (scratch, index_ref, sems) = rest[:-3], rest[-3:]
    moves = [
        (index_hbm, index_ref), (nodes_hbm, nodes_ref), (radial_hbm, radial_ref),
        (src_hbm, src_ref), (dst_hbm, dst_ref), (wig_hbm, wig_ref), (grads_hbm, grads_ref),
        (weight_hbm, weight_ref),
    ]
    copies = [pltpu.make_async_copy(a, b, sems.at[i]) for i, (a, b) in enumerate(moves)]
    for copy in copies:
        copy.start()
    copies[0].wait()
    copies[1].wait()
    coefs, atoms, _ = nodes_ref.shape
    scratch[coefs * atoms :, :] = jnp.zeros((scratch.shape[0] - coefs * atoms, scratch.shape[1]), F32)
    for coef in range(coefs):
        scratch[coef * atoms : (coef + 1) * atoms, :] = nodes_ref[coef].astype(F32)
    slot = index_ref.shape[0]
    for number, exchange in enumerate(plan):
        way, _ = ways_of(exchange)
        out, base = (outs[0], slot * number) if number < 2 else (outs[number - 1], 0)
        for place in range(slot):
            at = index_ref[place, way]
            out[base + place] = scratch[pl.ds(at, coefs, stride=atoms), :].astype(BF16)
    for copy in copies[2:]:
        copy.wait()


def expand_kernel(
    plan, slot, height, src_ref, dst_ref, wig_ref, grad_ref, nodes_ref, gr_ref, own_ref, *rest,
):
    to_own, to_halo, to_dst, wide = (*(rest[k * (LMAX + 1) : (k + 1) * (LMAX + 1)] for k in range(3)), rest[-1])
    node_dev = grad_ref.shape[1]
    edges = wig_ref.shape[3]
    dst = dst_hot(dst_ref[...], node_dev)
    src = src_hot(src_ref[...], node_dev, slot, [ways_of(x)[1] for x in plan], height)
    hots = [(to_own, src[:node_dev]), (to_halo, src[node_dev:]), (to_dst, dst)]
    for i in range(SIDE):
        for j in range(SIDE):
            start = (i * SIDE + j) * 8
            wide[start : start + LMAX + 1, :] = wig_ref[i, j].astype(F32)
    for degree in range(LMAX, -1, -1):
        width = 2 * degree + 1
        base = degree * degree
        for i in range(width):
            for j in range(width):
                at = (i * SIDE + j) * 8 + degree
                row = jnp.broadcast_to(wide[at : at + 1, :], (16, edges)).astype(BF16)
                for refs, hot in hots:
                    tall = hot.shape[0]
                    for start in range(0, tall, 16):
                        low = j * tall + start
                        refs[degree][low : low + 16, lanes(i, edges)] = hot[start : start + 16] * row
        atoms = jnp.concatenate([grad_ref[base + j] for j in range(width)], axis=0)
        gr = dot(atoms, to_dst[degree][...], 0, 0).astype(BF16)
        gr_ref[:, base * edges : (base + width) * edges] = gr
        atoms = jnp.concatenate([nodes_ref[base + j] for j in range(width)], axis=0)
        own = dot(atoms, to_own[degree][...], 0, 0).astype(BF16)
        own_ref[:, base * edges : (base + width) * edges] = own


def rot_kernel(slot, count_ref, radial_ref, gr_ref, own_ref, *rest):
    to_halo, (one, two, *more_halos) = rest[: LMAX + 1], rest[LMAX + 1 : -5]
    halos = [one.at[:slot], two, *more_halos]
    gain_ref, rot_ref, keep_ref, send_ref, scratch = rest[-5:]
    radial = radial_ref[...]
    at = lax.broadcasted_iota(jnp.int32, radial.shape, 1)
    gain = jnp.where(at < count_ref[0], radial, 0.0)
    gain_ref[...] = gain
    tall = scratch.shape[0] // ROW
    edges = rot_ref.shape[1] // COEF
    scratch[slot * len(halos) * ROW :, :] = jnp.zeros(
        ((tall - slot * len(halos)) * ROW, scratch.shape[1]), F32
    )
    for number, halo in enumerate(halos):
        for place in range(slot):
            start = (slot * number + place) * ROW
            scratch[start : start + COEF, :] = halo[place].astype(F32)
    for degree in range(LMAX, -1, -1):
        base, end = degree * degree, (degree + 1) * (degree + 1)
        span = slice(base * edges, end * edges)
        pieces = [scratch[pl.ds(coef, tall, stride=ROW), :].astype(BF16) for coef in range(base, end)]
        rot = dot(jnp.concatenate(pieces, axis=0), to_halo[degree][...], 0, 0).astype(BF16)
        rot_ref[:, span] = own_ref[:, span] + rot
    parts = []
    for order in range(LMAX + 1):
        coefs = order_coefs(order)
        left = side_by_side([rot_ref[:, lanes(k, edges)] for k in coefs])
        scale = gain[order : order + 1]
        right = side_by_side([(gr_ref[:, lanes(k, edges)].astype(F32) * scale).astype(BF16) for k in coefs])
        parts.append(dot(left, right, 1, 1))
    whole = jnp.concatenate(parts, axis=0)
    half = whole.shape[0] // 2
    first = lax.rem(lax.axis_index("shard"), 2) == 0
    keep_ref[...] = jnp.where(first, whole[:half], whole[half:])
    send_ref[...] = jnp.where(first, whole[half:], whole[:half]).astype(BF16)


def mixed(values_ref, weight_ref, gain, degree, forward, edges):
    base = degree * degree
    found = [None] * (2 * degree + 1)
    for order in range(degree + 1):
        places = places_of(degree, order)
        part = side_by_side([values_ref[:, lanes(base + i, edges)] for i in places])
        scale = side_by_side([gain[order : order + 1]] * len(places))
        out = (dot(weight_ref[order], part, 0 if forward else 1, 0) * scale).astype(BF16)
        for number, i in enumerate(places):
            found[i] = out[:, lanes(number, edges)]
    return side_by_side(found)


def back_kernel(gain_ref, weight_ref, gr_ref, *rest):
    to_own, to_halo, rest = rest[: LMAX + 1], rest[LMAX + 1 : 2 * LMAX + 2], rest[2 * LMAX + 2 :]
    own_ref, backs, scratch = rest[0], rest[1:-1], rest[-1]
    node_dev, tall = own_ref.shape[0] // COEF, scratch.shape[0] // ROW
    edges = gr_ref.shape[1] // COEF
    gain = gain_ref[...]
    scratch[...] = jnp.zeros(scratch.shape, F32)
    for degree in range(LMAX, -1, -1):
        base, width = degree * degree, 2 * degree + 1
        back = mixed(gr_ref, weight_ref, gain, degree, False, edges)
        out = dot(jnp.concatenate([to_own[degree][...], to_halo[degree][...]], axis=0), back, 1, 1)
        own_ref[base * node_dev : (base + width) * node_dev, :] = out[: width * node_dev]
        for j in range(width):
            low = width * node_dev + j * tall
            scratch[pl.ds(base + j, tall, stride=ROW), :] = out[low : low + tall]
    start = 0
    for back_ref in backs:
        back_ref[...] = scratch[start : start + back_ref.shape[0], :].astype(BF16)
        start += back_ref.shape[0]


def update_kernel(gain_ref, weight_ref, rot_ref, *rest):
    to_dst, out_ref = rest[:-1], rest[-1]
    node_dev = out_ref.shape[1]
    edges = rot_ref.shape[1] // COEF
    gain = gain_ref[...]
    for degree in range(LMAX, -1, -1):
        msg = mixed(rot_ref, weight_ref, gain, degree, True, edges)
        out = dot(to_dst[degree][...], msg, 1, 1).astype(BF16)
        for j in range(2 * degree + 1):
            out_ref[degree * degree + j] = out[j * node_dev : (j + 1) * node_dev]


def finish_kernel(plan, slot, index_ref, own_ref, *rest):
    (one, two, *backs), out_ref, scratch = rest[:-2], rest[-2], rest[-1]
    coefs, atoms, _ = out_ref.shape
    backs = [one.at[: slot * ROW], two.at[slot * ROW :], *backs]
    scratch[: coefs * atoms, :] = own_ref[...]
    for exchange, back in zip(plan, backs):
        way, _ = ways_of(exchange)
        for place in range(slot):
            at = index_ref[place, way]
            rows = scratch[pl.ds(at, coefs, stride=atoms), :]
            come = back[place * ROW : place * ROW + coefs, :].astype(F32)
            scratch[pl.ds(at, coefs, stride=atoms), :] = rows + come
    for coef in range(coefs):
        out_ref[coef] = scratch[coef * atoms : (coef + 1) * atoms, :].astype(BF16)


def join_kernel(mine_ref, other_ref, out_ref):
    half = mine_ref.shape[0]
    first = lax.rem(lax.axis_index("shard"), 2) == 0
    mine, other = mine_ref[...], other_ref[...]
    out_ref[:half, :] = jnp.where(first, mine, other)
    out_ref[half:, :] = jnp.where(first, other, mine)


VMEM = pl.BlockSpec(memory_space=pltpu.VMEM)
SMEM = pl.BlockSpec(memory_space=pltpu.SMEM)
HBM = pl.BlockSpec(memory_space=pltpu.HBM)


def call(kernel, ins, outs, scratch=(), flops=0, moved=0, vmem=32):
    return pl.pallas_call(
        kernel,
        in_specs=ins,
        out_specs=[VMEM] * len(outs),
        out_shape=outs,
        scratch_shapes=list(scratch),
        compiler_params=pltpu.CompilerParams(vmem_limit_bytes=vmem * 2**20),
        cost_estimate=pl.CostEstimate(flops=flops, bytes_accessed=moved, transcendentals=0),
    )


def total_of(keep, send, fills):
    groups, shards = lax.axis_size("group"), lax.axis_size("shard")
    both = ("group", "shard")
    along = [("shard", 1 << b) for b in range(1, shards.bit_length() - 1)]
    within = [("group", 1 << b) for b in range(groups.bit_length() - 1)]
    orders = [within + along, along + within]
    total = keep + lax.ppermute(send, "shard", [(s, s ^ 1) for s in range(shards)]).astype(F32)
    mine = total.astype(BF16)
    for step in range(len(orders[0])):
        if step:
            mine = (mine.astype(F32) + came.astype(F32)).astype(BF16)
        pairs = []
        for g in range(groups):
            for s in range(shards):
                axis, bit = orders[s % 2][step]
                to = (g ^ bit) * shards + s if axis == "group" else g * shards + (s ^ bit)
                pairs.append((g * shards + s, to))
        came = lax.ppermute(mine, both, pairs)
        for fill in fills.get(step, []):
            came = fill(mine, came)
    return mine.astype(F32) + came.astype(F32)


def per_device(plan, node_features, weight, wigner, radial, edge_src, edge_dst, send_index, edge_count, grad_update):
    node_dev, coefs, channels = node_features.shape
    slot = send_index.shape[1]
    edges = edge_src.shape[0]
    tall = -(-(slot * len(plan)) // 16) * 16
    height = node_dev + tall
    src, dst = edge_src.reshape(1, edges), edge_dst.reshape(1, edges)
    nodes = node_features.transpose(1, 0, 2)
    grads = grad_update.transpose(1, 0, 2)
    wig = wigner.transpose(1, 2, 0, 3)
    index = send_index.T
    shape = jax.ShapeDtypeStruct
    piece, pair = (shape((n * slot, coefs, channels), BF16) for n in (1, 2))
    atoms = shape((coefs, node_dev, channels), BF16)
    many = shape((channels, coefs * edges), BF16)
    wide = pltpu.VMEM((ROW * node_dev, channels), F32)

    inner = plan[2:]
    nodes, grads, wig, radials, src, dst, weights, *outgoing = call(
        functools.partial(stage_kernel, plan),
        [HBM] * 8,
        [shape(x.shape, x.dtype) for x in (nodes, grads, wig, radial, src, dst, weight)]
        + [pair] + [piece] * len(inner),
        [
            wide,
            pltpu.SMEM(index.shape, jnp.int32),
            pltpu.SemaphoreType.DMA((8,)),
        ],
        moved=400000,
        vmem=32,
    )(
        *[pltpu.with_memory_space_constraint(x, pltpu.HBM) for x in (index, nodes, grads, wig, radial, src, dst, weight)],
    )
    one, two = relay(outgoing[0])
    arrived = [lax.ppermute(x, e[0], e[5]) for x, e in zip(outgoing[1:], inner)]
    arrived = [one, two(), *arrived]

    widths = [2 * degree + 1 for degree in range(LMAX + 1)]
    gr, own_rot, *matrices = call(
        functools.partial(expand_kernel, plan, slot, height),
        [VMEM] * 5,
        [many, many]
        + [shape((width * n, width * edges), BF16) for n in (node_dev, tall, node_dev) for width in widths],
        [pltpu.VMEM((SIDE * SIDE * 8, edges), F32)],
        flops=3 * 10**9,
    )(src, dst, wig, grads, nodes)
    to_own, to_halo, to_dst = (matrices[k * (LMAX + 1) : (k + 1) * (LMAX + 1)] for k in range(3))

    half = shape((weight.shape[0] * channels // 2, channels), F32)
    gain, rot, keep, send = call(
        functools.partial(rot_kernel, slot),
        [SMEM] + [VMEM] * (3 + LMAX + 1 + len(plan)),
        [shape(radial.shape, F32), many, half, shape(half.shape, BF16)],
        [pltpu.VMEM((tall * ROW, channels), F32)],
        flops=3 * 10**9,
    )(edge_count, radials, gr, own_rot, *to_halo, *arrived)

    held = {}

    def run_back(mine, theirs):
        mine, late = lax.optimization_barrier((mine, gr))
        out = call(
            back_kernel,
            [VMEM] * (3 + 2 * (LMAX + 1)),
            [shape((coefs * node_dev, channels), F32), shape((2 * slot * ROW, channels), BF16)]
            + [shape((slot * ROW, channels), BF16)] * len(inner),
            [pltpu.VMEM((tall * ROW, channels), F32)],
            flops=3 * 10**9,
        )(gain, weights, late, *to_own, *to_halo)
        theirs, *out = lax.optimization_barrier((theirs, *out))
        held["own"], held["backs"] = out[0], out[1:]
        return theirs

    def run_update(mine, theirs):
        mine, late = lax.optimization_barrier((mine, rot))
        [out] = call(
            update_kernel, [VMEM] * (3 + LMAX + 1), [atoms], flops=3 * 10**9
        )(gain, weights, late, *to_dst)
        theirs, held["update"] = lax.optimization_barrier((theirs, out))
        return theirs

    returned = {}

    def go(number, x):
        if number < 2:
            return swapped(x, "group", 1 << number)
        return lax.ppermute(x, plan[number][0], plan[number][5])

    def run_returns(numbers):
        def run(mine, theirs):
            ready = [returned[0] if i == 1 else held["backs"][max(i - 1, 0)] for i in numbers]
            mine, *late = lax.optimization_barrier((mine, *ready))
            for i, x in zip(numbers, late):
                returned[i] = go(i, x)
            return theirs

        return run

    def end_returns(numbers):
        def run(mine, theirs):
            theirs, *came = lax.optimization_barrier((theirs, *[returned[i] for i in numbers]))
            for i, x in zip(numbers, came):
                returned[i] = x
            return theirs

        return run

    whole = range(len(plan))
    fills = {0: [run_back, run_returns([0])], 1: [run_returns(whole[2:]), end_returns([0])], 2: [run_returns([1]), end_returns(whole[2:])], 3: [end_returns([1]), run_update]}
    total = total_of(keep, send, fills)
    other = lax.ppermute(total, "shard", [(s, s ^ 1) for s in range(lax.axis_size("shard"))])
    [grad_weight] = call(
        join_kernel, [VMEM] * 2, [shape((2 * half.shape[0], channels), F32)], moved=10**6
    )(total, other)
    [grad_input] = call(
        functools.partial(finish_kernel, plan, slot),
        [SMEM] + [VMEM] * (1 + len(plan)),
        [atoms],
        [wide],
        moved=800000,
    )(index, held["own"], *[returned[i] for i in whole])
    return (
        held["update"].transpose(1, 0, 2),
        grad_input.transpose(1, 0, 2),
        grad_weight.reshape(weight.shape),
    )


def solution(mesh):
    plan = exchanges(mesh.shape["group"], mesh.shape["shard"])
    both = ("group", "shard")
    return jax.shard_map(
        functools.partial(per_device, plan),
        mesh=mesh,
        in_specs=(
            P(both, None, None),
            P(),
            P(None, None, None, both),
            P(None, both),
            P(both),
            P(both),
            P(both, None),
            P(both),
            P(both, None, None),
        ),
        out_specs=(P(both, None, None), P(both, None, None), P()),
        check_vma=False,
    )
```

```python
import functools

import jax
import jax.numpy as jnp
from jax import lax
from jax.experimental import pallas as pl
from jax.experimental.pallas import tpu as pltpu
from jax.sharding import PartitionSpec as P

F32, BF16 = jnp.float32, jnp.bfloat16
COLS = 8
LMAX = 6
COEF = (LMAX + 1) ** 2
SIDE = 2 * LMAX + 1
ROW = 56
way_list = [(-1, -1), (-1, 0), (-1, 1), (0, -1), (0, 1), (1, -1), (1, 0), (1, 1)]


def exchanges(groups, shards):
    rows = shards // COLS
    found = []
    for dr, dc in [(0, 1), (1, -1), (1, 0), (1, 1)]:
        by = COLS * dr + dc
        for parity in (0, 1):
            pairs = []
            for s in range(shards):
                r, c = s // COLS, s % COLS
                if (r if dr else c) % 2 == parity and r + dr < rows and 0 <= c + dc < COLS:
                    pairs += [(s, s + by), (s + by, s)]
            if pairs:
                plus = way_list.index((dr, dc))
                found.append(("shard", plus, 7 - plus, "row" if dr else "col", parity, pairs))
    found.sort(key=lambda e: e[5][0][1] - e[5][0][0] == 1 and e[4] == 0)
    if groups != 4:
        raise ValueError("for 4 groups")
    return [("group", 8, 9, "group", parity, None) for parity in (0, 1)] + found


def relay(x):
    one = swapped(x, "group", 1)
    return one, lambda: swapped(one[one.shape[0] // 2 :], "group", 2)


def swapped(x, axis, bit):
    return lax.ppermute(x, axis, [(i, i ^ bit) for i in range(lax.axis_size(axis))])


def ways_of(exchange):
    _, plus, minus, coordinate, parity, _ = exchange
    if coordinate == "group":
        place = lax.axis_index("group")
    elif coordinate == "row":
        place = lax.div(lax.axis_index("shard"), COLS)
    else:
        place = lax.rem(lax.axis_index("shard"), COLS)
    lower = lax.rem(place, 2) == parity
    return jnp.where(lower, plus, minus), jnp.where(lower, minus, plus)


def dot(a, b, ca, cb):
    return lax.dot_general(a, b, (((ca,), (cb,)), ((), ())), preferred_element_type=F32)


def order_coefs(order):
    found = []
    for degree in range(order, LMAX + 1):
        centre = degree * degree + degree
        found += [centre] if order == 0 else [centre - order, centre + order]
    return found


def lanes(coef, edges):
    return slice(coef * edges, (coef + 1) * edges)


def dst_hot(dst, node_dev):
    edges = dst.shape[1]
    return (lax.broadcasted_iota(jnp.int32, (node_dev, edges), 0) == dst).astype(F32).astype(BF16)


def src_hot(src, node_dev, slot, ways, height):
    edges = src.shape[1]
    row = lax.broadcasted_iota(jnp.int32, (height, edges), 0)
    code = jnp.where(row < node_dev, row, -1)
    for number, way in enumerate(ways):
        for place in range(slot):
            code = jnp.where(
                row == node_dev + slot * number + place, node_dev + slot * way + place, code
            )
    return (code == src).astype(F32).astype(BF16)


def places_of(degree, order):
    return [degree] if order == 0 else [degree - order, degree + order]


def side_by_side(pieces):
    return jnp.concatenate(pieces, axis=1)


def stage_kernel(
    plan, index_hbm, nodes_hbm, grads_hbm, wig_hbm, radial_hbm, src_hbm, dst_hbm, weight_hbm,
    nodes_ref, grads_ref, wig_ref, radial_ref, src_ref, dst_ref, weight_ref, *rest,
):
    outs, (scratch, index_ref, sems) = rest[:-3], rest[-3:]
    moves = [
        (index_hbm, index_ref), (nodes_hbm, nodes_ref), (radial_hbm, radial_ref),
        (src_hbm, src_ref), (dst_hbm, dst_ref), (wig_hbm, wig_ref), (grads_hbm, grads_ref),
        (weight_hbm, weight_ref),
    ]
    copies = [pltpu.make_async_copy(a, b, sems.at[i]) for i, (a, b) in enumerate(moves)]
    for copy in copies:
        copy.start()
    copies[0].wait()
    copies[1].wait()
    coefs, atoms, _ = nodes_ref.shape
    scratch[coefs * atoms :, :] = jnp.zeros((scratch.shape[0] - coefs * atoms, scratch.shape[1]), F32)
    for coef in range(coefs):
        scratch[coef * atoms : (coef + 1) * atoms, :] = nodes_ref[coef].astype(F32)
    slot = index_ref.shape[0]
    for number, exchange in enumerate(plan):
        way, _ = ways_of(exchange)
        out, base = (outs[0], slot * number) if number < 2 else (outs[number - 1], 0)
        for place in range(slot):
            at = index_ref[place, way]
            out[base + place] = scratch[pl.ds(at, coefs, stride=atoms), :].astype(BF16)
    for copy in copies[2:]:
        copy.wait()


def expand_kernel(
    plan, slot, height, src_ref, dst_ref, wig_ref, grad_ref, nodes_ref, gr_ref, own_ref, *rest,
):
    to_own, to_halo, to_dst, wide = (*(rest[k * (LMAX + 1) : (k + 1) * (LMAX + 1)] for k in range(3)), rest[-1])
    node_dev = grad_ref.shape[1]
    edges = wig_ref.shape[3]
    dst = dst_hot(dst_ref[...], node_dev)
    src = src_hot(src_ref[...], node_dev, slot, [ways_of(x)[1] for x in plan], height)
    hots = [(to_own, src[:node_dev]), (to_halo, src[node_dev:]), (to_dst, dst)]
    for i in range(SIDE):
        for j in range(SIDE):
            start = (i * SIDE + j) * 8
            wide[start : start + LMAX + 1, :] = wig_ref[i, j].astype(F32)
    for degree in range(LMAX, -1, -1):
        width = 2 * degree + 1
        base = degree * degree
        for i in range(width):
            for j in range(width):
                at = (i * SIDE + j) * 8 + degree
                row = jnp.broadcast_to(wide[at : at + 1, :], (16, edges)).astype(BF16)
                for refs, hot in hots:
                    tall = hot.shape[0]
                    for start in range(0, tall, 16):
                        low = j * tall + start
                        refs[degree][low : low + 16, lanes(i, edges)] = hot[start : start + 16] * row
        atoms = jnp.concatenate([grad_ref[base + j] for j in range(width)], axis=0)
        gr = dot(atoms, to_dst[degree][...], 0, 0).astype(BF16)
        gr_ref[:, base * edges : (base + width) * edges] = gr
        atoms = jnp.concatenate([nodes_ref[base + j] for j in range(width)], axis=0)
        own = dot(atoms, to_own[degree][...], 0, 0).astype(BF16)
        own_ref[:, base * edges : (base + width) * edges] = own


def rot_kernel(slot, count_ref, radial_ref, gr_ref, own_ref, *rest):
    to_halo, (one, two, *more_halos) = rest[: LMAX + 1], rest[LMAX + 1 : -5]
    halos = [one.at[:slot], two, *more_halos]
    gain_ref, rot_ref, keep_ref, send_ref, scratch = rest[-5:]
    radial = radial_ref[...]
    at = lax.broadcasted_iota(jnp.int32, radial.shape, 1)
    gain = jnp.where(at < count_ref[0], radial, 0.0)
    gain_ref[...] = gain
    tall = scratch.shape[0] // ROW
    edges = rot_ref.shape[1] // COEF
    scratch[slot * len(halos) * ROW :, :] = jnp.zeros(
        ((tall - slot * len(halos)) * ROW, scratch.shape[1]), F32
    )
    for number, halo in enumerate(halos):
        for place in range(slot):
            start = (slot * number + place) * ROW
            scratch[start : start + COEF, :] = halo[place].astype(F32)
    for degree in range(LMAX, -1, -1):
        base, end = degree * degree, (degree + 1) * (degree + 1)
        span = slice(base * edges, end * edges)
        pieces = [scratch[pl.ds(coef, tall, stride=ROW), :].astype(BF16) for coef in range(base, end)]
        rot = dot(jnp.concatenate(pieces, axis=0), to_halo[degree][...], 0, 0).astype(BF16)
        rot_ref[:, span] = own_ref[:, span] + rot
    parts = []
    for order in range(LMAX + 1):
        coefs = order_coefs(order)
        left = side_by_side([rot_ref[:, lanes(k, edges)] for k in coefs])
        scale = gain[order : order + 1]
        right = side_by_side([(gr_ref[:, lanes(k, edges)].astype(F32) * scale).astype(BF16) for k in coefs])
        parts.append(dot(left, right, 1, 1))
    whole = jnp.concatenate(parts, axis=0)
    half = whole.shape[0] // 2
    first = lax.rem(lax.axis_index("shard"), 2) == 0
    keep_ref[...] = jnp.where(first, whole[:half], whole[half:])
    send_ref[...] = jnp.where(first, whole[half:], whole[:half]).astype(BF16)


def mixed(values_ref, weight_ref, gain, degree, forward, edges):
    base = degree * degree
    found = [None] * (2 * degree + 1)
    for order in range(degree + 1):
        places = places_of(degree, order)
        part = side_by_side([values_ref[:, lanes(base + i, edges)] for i in places])
        scale = side_by_side([gain[order : order + 1]] * len(places))
        out = (dot(weight_ref[order], part, 0 if forward else 1, 0) * scale).astype(BF16)
        for number, i in enumerate(places):
            found[i] = out[:, lanes(number, edges)]
    return side_by_side(found)


def back_kernel(gain_ref, weight_ref, gr_ref, *rest):
    to_own, to_halo, rest = rest[: LMAX + 1], rest[LMAX + 1 : 2 * LMAX + 2], rest[2 * LMAX + 2 :]
    own_ref, backs, scratch = rest[0], rest[1:-1], rest[-1]
    node_dev, tall = own_ref.shape[0] // COEF, scratch.shape[0] // ROW
    edges = gr_ref.shape[1] // COEF
    gain = gain_ref[...]
    scratch[...] = jnp.zeros(scratch.shape, F32)
    for degree in range(LMAX, -1, -1):
        base, width = degree * degree, 2 * degree + 1
        back = mixed(gr_ref, weight_ref, gain, degree, False, edges)
        out = dot(jnp.concatenate([to_own[degree][...], to_halo[degree][...]], axis=0), back, 1, 1)
        own_ref[base * node_dev : (base + width) * node_dev, :] = out[: width * node_dev]
        for j in range(width):
            low = width * node_dev + j * tall
            scratch[pl.ds(base + j, tall, stride=ROW), :] = out[low : low + tall]
    start = 0
    for back_ref in backs:
        back_ref[...] = scratch[start : start + back_ref.shape[0], :].astype(BF16)
        start += back_ref.shape[0]


def update_kernel(gain_ref, weight_ref, rot_ref, *rest):
    to_dst, out_ref = rest[:-1], rest[-1]
    node_dev = out_ref.shape[1]
    edges = rot_ref.shape[1] // COEF
    gain = gain_ref[...]
    for degree in range(LMAX, -1, -1):
        msg = mixed(rot_ref, weight_ref, gain, degree, True, edges)
        out = dot(to_dst[degree][...], msg, 1, 1).astype(BF16)
        for j in range(2 * degree + 1):
            out_ref[degree * degree + j] = out[j * node_dev : (j + 1) * node_dev]


def finish_kernel(plan, slot, index_ref, own_ref, *rest):
    (one, two, *backs), out_ref, scratch = rest[:-2], rest[-2], rest[-1]
    coefs, atoms, _ = out_ref.shape
    backs = [one.at[: slot * ROW], two.at[slot * ROW :], *backs]
    scratch[: coefs * atoms, :] = own_ref[...]
    for exchange, back in zip(plan, backs):
        way, _ = ways_of(exchange)
        for place in range(slot):
            at = index_ref[place, way]
            rows = scratch[pl.ds(at, coefs, stride=atoms), :]
            come = back[place * ROW : place * ROW + coefs, :].astype(F32)
            scratch[pl.ds(at, coefs, stride=atoms), :] = rows + come
    for coef in range(coefs):
        out_ref[coef] = scratch[coef * atoms : (coef + 1) * atoms, :].astype(BF16)


def join_kernel(mine_ref, other_ref, out_ref):
    half = mine_ref.shape[0]
    first = lax.rem(lax.axis_index("shard"), 2) == 0
    mine, other = mine_ref[...], other_ref[...]
    out_ref[:half, :] = jnp.where(first, mine, other)
    out_ref[half:, :] = jnp.where(first, other, mine)


VMEM = pl.BlockSpec(memory_space=pltpu.VMEM)
SMEM = pl.BlockSpec(memory_space=pltpu.SMEM)
HBM = pl.BlockSpec(memory_space=pltpu.HBM)


def call(kernel, ins, outs, scratch=(), flops=0, moved=0, vmem=32):
    return pl.pallas_call(
        kernel,
        in_specs=ins,
        out_specs=[VMEM] * len(outs),
        out_shape=outs,
        scratch_shapes=list(scratch),
        compiler_params=pltpu.CompilerParams(vmem_limit_bytes=vmem * 2**20),
        cost_estimate=pl.CostEstimate(flops=flops, bytes_accessed=moved, transcendentals=0),
    )


def total_of(keep, send, fills):
    groups, shards = lax.axis_size("group"), lax.axis_size("shard")
    both = ("group", "shard")
    along = [("shard", 1 << b) for b in range(1, shards.bit_length() - 1)]
    within = [("group", 1 << b) for b in range(groups.bit_length() - 1)]
    orders = [within[:1] + along[1:] + within[1:] + along[:1], along[1:] + within[:1] + along[:1] + within[1:]]
    total = keep + lax.ppermute(send, "shard", [(s, s ^ 1) for s in range(shards)]).astype(F32)
    mine = total.astype(BF16)
    for step in range(len(orders[0])):
        if step:
            mine = (mine.astype(F32) + came.astype(F32)).astype(BF16)
        pairs = []
        for g in range(groups):
            for s in range(shards):
                axis, bit = orders[s % 2][step]
                to = (g ^ bit) * shards + s if axis == "group" else g * shards + (s ^ bit)
                pairs.append((g * shards + s, to))
        came = lax.ppermute(mine, both, pairs)
        for fill in fills.get(step, []):
            came = fill(mine, came)
    return mine.astype(F32) + came.astype(F32)


def per_device(plan, node_features, weight, wigner, radial, edge_src, edge_dst, send_index, edge_count, grad_update):
    node_dev, coefs, channels = node_features.shape
    slot = send_index.shape[1]
    edges = edge_src.shape[0]
    tall = -(-(slot * len(plan)) // 16) * 16
    height = node_dev + tall
    src, dst = edge_src.reshape(1, edges), edge_dst.reshape(1, edges)
    nodes = node_features.transpose(1, 0, 2)
    grads = grad_update.transpose(1, 0, 2)
    wig = wigner.transpose(1, 2, 0, 3)
    index = send_index.T
    shape = jax.ShapeDtypeStruct
    piece, pair = (shape((n * slot, coefs, channels), BF16) for n in (1, 2))
    atoms = shape((coefs, node_dev, channels), BF16)
    many = shape((channels, coefs * edges), BF16)
    wide = pltpu.VMEM((ROW * node_dev, channels), F32)

    inner = plan[2:]
    nodes, grads, wig, radials, src, dst, weights, *outgoing = call(
        functools.partial(stage_kernel, plan),
        [HBM] * 8,
        [shape(x.shape, x.dtype) for x in (nodes, grads, wig, radial, src, dst, weight)]
        + [pair] + [piece] * len(inner),
        [
            wide,
            pltpu.SMEM(index.shape, jnp.int32),
            pltpu.SemaphoreType.DMA((8,)),
        ],
        moved=400000,
        vmem=32,
    )(
        *[pltpu.with_memory_space_constraint(x, pltpu.HBM) for x in (index, nodes, grads, wig, radial, src, dst, weight)],
    )
    one, two = relay(outgoing[0])
    arrived = [lax.ppermute(x, e[0], e[5]) for x, e in zip(outgoing[1:], inner)]
    arrived = [one, two(), *arrived]

    widths = [2 * degree + 1 for degree in range(LMAX + 1)]
    gr, own_rot, *matrices = call(
        functools.partial(expand_kernel, plan, slot, height),
        [VMEM] * 5,
        [many, many]
        + [shape((width * n, width * edges), BF16) for n in (node_dev, tall, node_dev) for width in widths],
        [pltpu.VMEM((SIDE * SIDE * 8, edges), F32)],
        flops=3 * 10**9,
    )(src, dst, wig, grads, nodes)
    to_own, to_halo, to_dst = (matrices[k * (LMAX + 1) : (k + 1) * (LMAX + 1)] for k in range(3))

    half = shape((weight.shape[0] * channels // 2, channels), F32)
    gain, rot, keep, send = call(
        functools.partial(rot_kernel, slot),
        [SMEM] + [VMEM] * (3 + LMAX + 1 + len(plan)),
        [shape(radial.shape, F32), many, half, shape(half.shape, BF16)],
        [pltpu.VMEM((tall * ROW, channels), F32)],
        flops=3 * 10**9,
    )(edge_count, radials, gr, own_rot, *to_halo, *arrived)

    held = {}

    def run_back(mine, theirs):
        mine, late = lax.optimization_barrier((mine, gr))
        out = call(
            back_kernel,
            [VMEM] * (3 + 2 * (LMAX + 1)),
            [shape((coefs * node_dev, channels), F32), shape((2 * slot * ROW, channels), BF16)]
            + [shape((slot * ROW, channels), BF16)] * len(inner),
            [pltpu.VMEM((tall * ROW, channels), F32)],
            flops=3 * 10**9,
        )(gain, weights, late, *to_own, *to_halo)
        theirs, *out = lax.optimization_barrier((theirs, *out))
        held["own"], held["backs"] = out[0], out[1:]
        return theirs

    def run_update(mine, theirs):
        mine, late = lax.optimization_barrier((mine, rot))
        [out] = call(
            update_kernel, [VMEM] * (3 + LMAX + 1), [atoms], flops=3 * 10**9
        )(gain, weights, late, *to_dst)
        theirs, held["update"] = lax.optimization_barrier((theirs, out))
        return theirs

    returned = {}

    def go(number, x):
        if number < 2:
            return swapped(x, "group", 1 << number)
        return lax.ppermute(x, plan[number][0], plan[number][5])

    def run_returns(numbers):
        def run(mine, theirs):
            ready = [returned[0] if i == 1 else held["backs"][max(i - 1, 0)] for i in numbers]
            mine, *late = lax.optimization_barrier((mine, *ready))
            for i, x in zip(numbers, late):
                returned[i] = go(i, x)
            return theirs

        return run

    def end_returns(numbers):
        def run(mine, theirs):
            theirs, *came = lax.optimization_barrier((theirs, *[returned[i] for i in numbers]))
            for i, x in zip(numbers, came):
                returned[i] = x
            return theirs

        return run

    whole = range(len(plan))
    fills = {0: [run_back, run_returns([0])], 1: [run_returns(whole[2:]), end_returns([0])], 2: [run_returns([1]), run_update, end_returns(whole[2:])], 3: [end_returns([1])]}
    total = total_of(keep, send, fills)
    other = lax.ppermute(total, "shard", [(s, s ^ 1) for s in range(lax.axis_size("shard"))])
    [grad_weight] = call(
        join_kernel, [VMEM] * 2, [shape((2 * half.shape[0], channels), F32)], moved=10**6
    )(total, other)
    [grad_input] = call(
        functools.partial(finish_kernel, plan, slot),
        [SMEM] + [VMEM] * (1 + len(plan)),
        [atoms],
        [wide],
        moved=800000,
    )(index, held["own"], *[returned[i] for i in whole])
    return (
        held["update"].transpose(1, 0, 2),
        grad_input.transpose(1, 0, 2),
        grad_weight.reshape(weight.shape),
    )


def solution(mesh):
    plan = exchanges(mesh.shape["group"], mesh.shape["shard"])
    both = ("group", "shard")
    return jax.shard_map(
        functools.partial(per_device, plan),
        mesh=mesh,
        in_specs=(
            P(both, None, None),
            P(),
            P(None, None, None, both),
            P(None, both),
            P(both),
            P(both),
            P(both, None),
            P(both),
            P(both, None, None),
        ),
        out_specs=(P(both, None, None), P(both, None, None), P()),
        check_vma=False,
    )
```
